32 devices in a mesh: dp: 8 (over y, x, core), head: 4 (over z).
Axes of the slice: x: 2, y: 2, z: 4, core: 2. Of those that a mesh axis runs over, the one named last changes fastest.
Arguments:
- tile_features: bfloat16 [16, 1601, 7680], P('dp', None, 'head'), may hold values from -6 to 6
- projection: bfloat16 [7680, 8, 256], P('head'), may hold values from -0.09375 to 0.09375
- queries: bfloat16 [8, 64, 8192], P('dp', None, 'head'), may hold values from -36 to 36
- query_gain: float32 [128], replicated, may hold values from 1 to 2.2
- key_gain: float32 [128], replicated, may hold values from 1 to 2.2
- tile_count: int32 [8], P('dp'), may hold values from 1 to 4, as said below
- tile_slot: int32 [8, 4], P('dp'), may hold values from 0 to 15, as said below
- cross_mask: int32 [8, 64, 4], P('dp'), may hold values 0 or 1
- prompt_length: int32 [8], P('dp'), may hold values from 16 to 64, as said below
Outputs:
- context: bfloat16 [8, 64, 8192], P('dp', None, 'head')
The draws below stay inside these ranges and needn't reach their ends.
Inputs may be any that keep to these rules, and one draw needn't show every extreme that they name: `tile_count`: the counts of each aligned group of 4 requests sum to 8; some request has 4 tiles and some has one. Slot s sits on index s // 2 of dp; every slot holds exactly one tile; for t < tile_count[r], tile_slot[r, t] is the slot of tile t of request r, one of the 8 slots of the aligned group of 4 indices of dp that holds request r; entries with t >= tile_count[r] are arbitrary slots. `prompt_length`: some request uses all 64 rows.
All inputs are finite; a program needn't handle non-finite values. No bound on the sum of `cross_mask` on one device may be relied on, other than what follows from the above.
Results may differ from the reference program's by a relative error of at most 0.04.
Values may be sent and summed in bfloat16 or wider, within the bound.
A program may use at most 128 MiB of HBM per device.

```python
import math
import jax
import jax.numpy as jnp
import numpy as np
from jax import lax

VDIM = 7680
HEADS = 64
KVH = 8
HD = 128
TROWS = 1601
MAXT = 4
TILES_DEV = 2
GROUP = 4
PROMPT = 64
REQUESTS = 8
SLOTS = 16
N_HEAD = 4


def count_rows():
    combos = np.arange(MAXT ** GROUP)
    powers = MAXT ** np.arange(GROUP)
    grid = combos[:, None] // powers[None, :] % MAXT + 1
    kept_rows = grid[grid.sum(axis=1) == GROUP * TILES_DEV]
    return jnp.asarray(kept_rows, dtype=jnp.int32)


def tile_layout(key):
    groups = REQUESTS // GROUP
    group_slots = GROUP * TILES_DEV
    table = count_rows()
    chosen = jax.random.randint(jax.random.fold_in(key, 11), (groups,), 0, table.shape[0])
    counts = table[chosen]
    forced_group = jax.random.randint(jax.random.fold_in(key, 12), (), 0, groups)
    forced = jax.random.permutation(jax.random.fold_in(key, 13), jnp.array([MAXT, 1, 1, group_slots - MAXT - 2], dtype=jnp.int32))
    counts = jnp.where((jnp.arange(groups) == forced_group)[:, None], forced[None, :], counts)
    shuffle_keys = jax.random.split(jax.random.fold_in(key, 14), groups)
    shuffles = jax.vmap(lambda one_key: jax.random.permutation(one_key, group_slots))(shuffle_keys).astype(jnp.int32)
    starts = jnp.cumsum(counts, axis=1) - counts
    tile_range = jnp.arange(MAXT, dtype=jnp.int32)
    positions = jnp.minimum(starts[:, :, None] + tile_range[None, None, :], group_slots - 1)
    picked = jnp.take_along_axis(shuffles, positions.reshape(groups, GROUP * MAXT), axis=1).reshape(groups, GROUP, MAXT)
    slots = picked + (jnp.arange(groups, dtype=jnp.int32) * group_slots)[:, None, None]
    usable = tile_range[None, None, :] < counts[:, :, None]
    filler = jax.random.randint(jax.random.fold_in(key, 15), (groups, GROUP, MAXT), 0, SLOTS)
    tile_slot = jnp.where(usable, slots, filler).reshape(REQUESTS, MAXT).astype(jnp.int32)
    return (counts.reshape(REQUESTS).astype(jnp.int32), tile_slot)


def draw_tile_count(key, part):
    counts, slots = tile_layout(key)
    return counts


def draw_tile_slot(key, part):
    counts, slots = tile_layout(key)
    return slots


def draw_prompt_length(key, part):
    key = jax.random.fold_in(key, 3)
    lengths = jax.random.randint(jax.random.fold_in(key, 1), (REQUESTS,), PROMPT // 4, PROMPT + 1)
    full_index = jax.random.randint(jax.random.fold_in(key, 2), (), 0, REQUESTS)
    return jnp.where(jnp.arange(REQUESTS) == full_index, PROMPT, lengths).astype(jnp.int32)


def draw_queries(key, part):
    key = jax.random.fold_in(key, 4)
    shape = (REQUESTS, PROMPT, HEADS * HD)
    row_scale = jnp.exp(jax.random.uniform(jax.random.fold_in(key, 1), (REQUESTS, PROMPT, 1), minval=math.log(0.3), maxval=math.log(3.0)))
    column_scale = jnp.exp(jax.random.uniform(jax.random.fold_in(key, 2), (1, 1, HEADS * HD), minval=math.log(0.3), maxval=math.log(3.0)))
    normal_part = jnp.clip(jax.random.normal(jax.random.fold_in(key, 3), shape), -4.0, 4.0)
    return (normal_part * row_scale * column_scale).astype(jnp.bfloat16)


def with_ends(entries, stream_key, least, high):
    index_at = [jax.random.randint(jax.random.fold_in(stream_key, axis), (), 0, length) for axis, length in enumerate(entries.shape)]
    widest = entries.shape.index(max(entries.shape))
    beside = index_at[:widest] + [(index_at[widest] + 1) % entries.shape[widest]] + index_at[widest + 1:]
    return entries.at[tuple(index_at)].set(least).at[tuple(beside)].set(high)


def raised(values, stream_key, source, target, parts, factor):
    def block_of(axis_at):
        return (jnp.arange(values.shape[axis_at]) // (values.shape[axis_at] // parts)).reshape((-1,) + (1,) * (values.ndim - 1 - axis_at))

    first = jax.random.permutation(stream_key, parts)[block_of(target)]
    other_side = (block_of(target) + parts // 2) % parts
    return jnp.where((block_of(source) == first) | (block_of(source) == other_side), factor * values, values)


def block_levels(key, dims, shards, low, largest):
    factor_of = 1.0
    for dim, blocks in shards:
        draws = jax.random.uniform(jax.random.fold_in(jax.random.fold_in(key, 6), dim), (blocks,), jnp.float32, low / len(shards), largest / len(shards))
        factor_of = factor_of * jnp.repeat(jnp.exp(draws), dims[dim] // blocks).reshape((-1,) + (1,) * (len(dims) - 1 - dim))
    return factor_of


def scatter_about(own_key, shape, spread, most, cuts=(), held_as=jnp.bfloat16):
    values = jax.random.normal(own_key, shape, jnp.float32) * spread
    if len(cuts) > 0:
        values = block_levels(own_key, shape, cuts, -0.22, 0.18) * values
    return jnp.clip(values, min=-most, max=most).astype(held_as)


def gaussian_with(key, dims, width, reach, shards, heavy, held_as=jnp.bfloat16):
    values = width * jax.random.normal(key, dims, jnp.float32)
    if shards:
        values = values * block_levels(key, dims, shards, -0.22, 0.18)
    return jnp.clip(raised(values, jax.random.fold_in(key, 3), *heavy), -reach, reach).astype(held_as)


def setup_inputs(seed: int = 0) -> dict:
    streams_of = jax.random.split(jax.random.key(seed), 10)
    return {
        "tile_features": scatter_about(streams_of[0], (SLOTS, TROWS, VDIM), 1.0, 6.0, ((0, 8), (2, 4))),
        "projection": gaussian_with(streams_of[1], (VDIM, KVH, 2 * HD), VDIM ** -0.5, 0.09375, ((0, 4),), (0, 1, 4, 2.0)),
        "queries": draw_queries(jax.random.fold_in(streams_of[9], 71), 0),
        "query_gain": jnp.clip(jnp.exp(jax.random.uniform(streams_of[3], (HD,), jnp.float32, math.log(1.0), math.log(2.2))), 1.0, 2.2),
        "key_gain": jnp.clip(jnp.exp(jax.random.uniform(streams_of[4], (HD,), jnp.float32, math.log(1.0), math.log(2.2))), 1.0, 2.2),
        "tile_count": draw_tile_count(jax.random.fold_in(streams_of[9], 71), 0),
        "tile_slot": draw_tile_slot(jax.random.fold_in(streams_of[9], 71), 0),
        "cross_mask": with_ends((jax.random.randint(streams_of[7], (REQUESTS, PROMPT, MAXT), 0, 4) < 3).astype(jnp.int32), jax.random.fold_in(streams_of[7], 1), 0, 1),
        "prompt_length": draw_prompt_length(jax.random.fold_in(streams_of[9], 71), 0),
    }


def round_half(values):
    return lax.optimization_barrier(values.astype(jnp.bfloat16))

def normalize_rows(values, row_gain):
    squares = lax.optimization_barrier(jnp.mean(values * values, axis=-1, keepdims=True))
    return values * lax.rsqrt(squares + 1e-05) * row_gain

def reference(tile_features, projection, queries, query_gain, key_gain, tile_count, tile_slot, cross_mask, prompt_length):
    group_width = VDIM // N_HEAD
    group_size = HEADS // KVH
    flat_rows = tile_features.reshape(SLOTS * TROWS, VDIM)
    flat_weight = projection.reshape(VDIM, KVH * 2 * HD)

    def add_group(group_index, running):
        first_column = (group_index * group_width).astype(jnp.int32)
        columns = lax.dynamic_slice_in_dim(flat_rows, first_column, group_width, 1)
        weight_rows = lax.dynamic_slice_in_dim(flat_weight, first_column, group_width, 0)
        partial_value = jnp.dot(columns, weight_rows, preferred_element_type=jnp.float32)
        return running + round_half(partial_value).astype(jnp.float32)
    running = lax.fori_loop(0, N_HEAD, add_group, jnp.zeros((SLOTS * TROWS, KVH * 2 * HD), jnp.float32))
    kv_tiles = round_half(running).reshape(SLOTS, TROWS, KVH, 2 * HD)
    keys_normed = round_half(normalize_rows(kv_tiles[..., :HD].astype(jnp.float32), key_gain))
    tile_values = kv_tiles[..., HD:]
    query_heads = queries.reshape(REQUESTS, PROMPT, KVH, group_size, HD)
    queries_normed = round_half(normalize_rows(query_heads.astype(jnp.float32), query_gain))
    score_scale = 1.0 / math.sqrt(HD)
    row_index = jnp.arange(PROMPT, dtype=jnp.int32)
    tile_range = jnp.arange(MAXT, dtype=jnp.int32)

    def attend(inputs):
        query_block, own_count, own_slots, own_mask, own_length = inputs
        numerator = jnp.zeros((PROMPT, KVH, group_size, HD), jnp.float32)
        denominator = jnp.zeros((PROMPT, KVH, group_size), jnp.float32)
        for tile_pos in range(MAXT):
            slot_here = own_slots[tile_pos].astype(jnp.int32)
            key_tile = lax.dynamic_index_in_dim(keys_normed, slot_here, 0, keepdims=False)
            value_tile = lax.dynamic_index_in_dim(tile_values, slot_here, 0, keepdims=False)
            scores = jnp.einsum('pkgd,nkd->pkgn', query_block.astype(jnp.float32), key_tile.astype(jnp.float32)) * score_scale
            usable = (own_mask[:, tile_pos] == 1) & (tile_pos < own_count) & (row_index < own_length)
            weights = round_half(jnp.where(usable[:, None, None, None], jnp.exp(scores), 0.0)).astype(jnp.float32)
            denominator = denominator + lax.optimization_barrier(jnp.sum(weights, axis=-1))
            numerator = numerator + jnp.einsum('pkgn,nkd->pkgd', weights, value_tile.astype(jnp.float32))
        live_rows = (row_index < own_length) & jnp.any((own_mask == 1) & (tile_range[None, :] < own_count), axis=1)
        divisor = jnp.where(live_rows[:, None, None], denominator, 1.0)
        result = jnp.where(live_rows[:, None, None, None], numerator / divisor[..., None], 0.0)
        return result.reshape(PROMPT, HEADS * HD).astype(jnp.bfloat16)
    return lax.map(attend, (queries_normed, tile_count, tile_slot, cross_mask, prompt_length))
```

```python
import math

import jax
import jax.numpy as jnp
from jax import lax
from jax.experimental import pallas as pl
from jax.experimental.pallas import tpu as pltpu
from jax.sharding import PartitionSpec as P

HEADS = 64
KVH = 8
HD = 128
MAXT = 4
GROUP = 4
NZ = 4
SLOTS_HERE = 2
ROWS = 320
UNIT = 5
LANES = 512
SKEW = 2
KHALF = KVH // 2
PER_K = SLOTS_HERE * UNIT
STEPS = KHALF * PER_K
LAST = (NZ - 1) * SKEW
MESH = pl.DeviceIdType.MESH
F32 = jnp.float32
BF16 = jnp.bfloat16


def weight_head(direction, kk):
    return KHALF + kk if direction == 0 else (kk + 2) % KHALF


def kernel(
    feat, tail, weight, query, qgain, kgain, meta, out,
    fbuf, wbuf, acc, tacc, qall, mall, qcur, num, den, csum, dsum, sbuf, rbuf, obuf, nbuf,
    fsem, wsem, csend, crecv, tsend, trecv, qzs, qzr, qfs, qfr, ms, mr, ss, sr, os_, or_,
):
    dp = lax.axis_index("dp")
    z = lax.axis_index("head")
    g = lax.rem(dp, GROUP)
    base = dp - g
    is_end = (z == 0) | (z == NZ - 1)
    peers = [lax.rem(g + o, GROUP) for o in range(1, GROUP)]
    sources = [lax.rem(g + GROUP - o, GROUP) for o in range(1, GROUP)]
    beside = jnp.where(z == 0, 1, jnp.where(z == 1, 0, jnp.where(z == 2, 3, 2)))
    final = jnp.where(z == 0, 1, 0)

    def weight_copy(direction, kk):
        return pltpu.make_async_copy(
            weight.at[weight_head(direction, kk)], wbuf.at[direction, kk], wsem.at[direction, kk]
        )

    def feat_copy(i):
        s, c = i // UNIT, lax.rem(i, UNIT)
        rows = pl.ds(pl.multiple_of(c * ROWS, ROWS), ROWS)
        return pltpu.make_async_copy(feat.at[s, rows], fbuf.at[s, c], fsem.at[i])

    for direction in range(2):
        weight_copy(direction, 0).start()
    for i in range(PER_K):
        feat_copy(i).start()
    for kk in range(1, KHALF):
        for direction in range(2):
            weight_copy(direction, kk).start()

    barrier = pltpu.get_barrier_semaphore()
    for p in peers:
        pl.semaphore_signal(barrier, inc=1, device_id={"dp": base + p}, device_id_type=MESH)

    @pl.when(z > 0)
    def _():
        pl.semaphore_signal(barrier, inc=1, device_id={"head": z - 1}, device_id_type=MESH)

    @pl.when(z < NZ - 1)
    def _():
        pl.semaphore_signal(barrier, inc=1, device_id={"head": z + 1}, device_id_type=MESH)

    for h in range(2 * KVH):
        block = query[0, :, h * HD:(h + 1) * HD].astype(F32)
        squares = jnp.mean(block * block, axis=-1, keepdims=True)
        normed = block * lax.rsqrt(squares + 1e-05) * qgain[...]
        qall[g, 2 + h // 8, (h % 8) * 64:(h % 8 + 1) * 64, :] = normed.astype(BF16)
    mall[g] = meta[...]

    @pl.when(is_end)
    def _():
        pl.semaphore_wait(barrier, GROUP)

    @pl.when(jnp.logical_not(is_end))
    def _():
        pl.semaphore_wait(barrier, GROUP + 1)

    def q_up(dst_half, row):
        return pltpu.make_async_remote_copy(
            src_ref=qall.at[row, pl.ds(2, 2)], dst_ref=qall.at[row, pl.ds(dst_half, 2)],
            send_sem=qzs, recv_sem=qzr, device_id={"head": beside}, device_id_type=MESH,
        )

    def q_forward(half, o, row):
        return pltpu.make_async_remote_copy(
            src_ref=qall.at[row, pl.ds(2 * half, 2)], dst_ref=qall.at[row, pl.ds(2 * half, 2)],
            send_sem=qfs.at[half, o], recv_sem=qfr.at[half, o],
            device_id={"dp": base + peers[o]}, device_id_type=MESH,
        )

    def meta_forward(o, row):
        return pltpu.make_async_remote_copy(
            src_ref=mall.at[row], dst_ref=mall.at[row], send_sem=ms.at[o], recv_sem=mr.at[o],
            device_id={"dp": base + peers[o]}, device_id_type=MESH,
        )

    def part_send(kk, o, src_row, dst_row):
        return pltpu.make_async_remote_copy(
            src_ref=sbuf.at[kk, src_row], dst_ref=rbuf.at[kk, dst_row],
            send_sem=ss.at[kk, o], recv_sem=sr.at[kk, o],
            device_id={"dp": base + peers[o]}, device_id_type=MESH,
        )

    def out_send():
        return pltpu.make_async_remote_copy(
            src_ref=obuf.at[pl.ds(0, 2)], dst_ref=nbuf, send_sem=os_, recv_sem=or_,
            device_id={"head": beside}, device_id_type=MESH,
        )

    @pl.when(jnp.logical_not(is_end))
    def _():
        q_up(0, g).start()

    @pl.when(is_end)
    def _():
        for o in range(GROUP - 1):
            meta_forward(o, g).start()
            q_forward(1, o, g).start()

    def chain(direction, i):
        step = 1 if direction == 0 else -1
        return pltpu.make_async_remote_copy(
            src_ref=acc.at[direction, i], dst_ref=acc.at[direction, i],
            send_sem=csend.at[direction, i], recv_sem=crecv.at[direction, i],
            device_id={"head": z + step}, device_id_type=MESH,
        )

    def tail_chain(direction, kk):
        step = 1 if direction == 0 else -1
        return pltpu.make_async_remote_copy(
            src_ref=tacc.at[direction, kk], dst_ref=tacc.at[direction, kk],
            send_sem=tsend.at[direction, kk], recv_sem=trecv.at[direction, kk],
            device_id={"head": z + step}, device_id_type=MESH,
        )

    def add_link(direction, i):
        first = (z == 0) if direction == 0 else (z == NZ - 1)
        last = (z == NZ - 1) if direction == 0 else (z == 0)
        kk = i // PER_K
        s = lax.rem(i, PER_K) // UNIT
        c = lax.rem(i, UNIT)

        @pl.when(lax.rem(i, PER_K) == 0)
        def _():
            part = jnp.dot(tail[...], wbuf[direction, kk], preferred_element_type=F32)

            @pl.when(first)
            def _():
                tacc[direction, kk] = part.astype(BF16)

            @pl.when(jnp.logical_not(first))
            def _():
                tail_chain(direction, kk).wait_recv()
                tacc[direction, kk] = (tacc[direction, kk].astype(F32) + part).astype(BF16)

            @pl.when(jnp.logical_not(last))
            def _():
                tail_chain(direction, kk).start()

        part = jnp.dot(fbuf[s, c], wbuf[direction, kk], preferred_element_type=F32)

        @pl.when(first)
        def _():
            acc[direction, i] = part.astype(BF16)

        @pl.when(jnp.logical_not(first))
        def _():
            chain(direction, i).wait_recv()
            acc[direction, i] = (acc[direction, i].astype(F32) + part).astype(BF16)

        @pl.when(jnp.logical_not(last))
        def _():
            chain(direction, i).start()

    def weigh(kv, valid):
        keys = kv[:, :HD].astype(F32)
        squares = jnp.mean(keys * keys, axis=-1, keepdims=True)
        normed = (keys * lax.rsqrt(squares + 1e-05) * kgain[...]).astype(BF16)
        scores = lax.dot_general(
            normed, qcur[...], (((1,), (1,)), ((), ())), preferred_element_type=F32
        ) * (1.0 / math.sqrt(HD))
        weights = jnp.exp(scores)
        if valid is not None:
            weights = jnp.where(valid, weights, 0.0)
        weights = weights.astype(BF16)
        denominator = jnp.sum(weights.astype(F32), axis=0, keepdims=True)
        numerator = lax.dot_general(
            kv[:, HD:], weights, (((0,), (0,)), ((), ())), preferred_element_type=F32
        )
        return numerator, denominator

    def hits(j, s):
        rows = mall[j]
        hit = jnp.where(rows[MAXT:2 * MAXT] == dp * SLOTS_HERE + s, 1, 0)
        match = jnp.max(hit, axis=0, keepdims=True)
        usable = jnp.max(hit * rows[:MAXT], axis=0, keepdims=True)
        return match, usable

    def attend(d):
        kk = d // PER_K
        s = lax.rem(d, PER_K) // UNIT

        @pl.when(lax.rem(d, UNIT) == 0)
        def _():
            chosen = jnp.zeros((LANES, HD), F32)
            for j in range(GROUP):
                match, _u = hits(j, s)
                chosen = chosen + match[:, :HD].astype(F32) * qall[j, kk].astype(F32)
            qcur[...] = chosen.astype(BF16)
            row = lax.broadcasted_iota(jnp.int32, (16, LANES), 0)
            n0, d0 = weigh(tacc[final, kk], row == s)
            num[...] = n0
            den[...] = d0

        n1, d1 = weigh(acc[final, d], None)
        num[...] += n1
        den[...] += d1

        @pl.when(lax.rem(d, PER_K) == UNIT - 1)
        def _():
            for j in range(GROUP):
                _m, usable = hits(j, s)
                csum[j] = jnp.where(usable == 1, num[...], 0.0)
                dsum[j] = jnp.where(usable == 1, den[...], 0.0)

        @pl.when(lax.rem(d, PER_K) == PER_K - 1)
        def _():
            for j in range(GROUP):
                _m, usable = hits(j, s)
                total = csum[j] + jnp.where(usable == 1, num[...], 0.0)
                below = dsum[j] + jnp.where(usable == 1, den[...], 0.0)
                high = below.astype(BF16).astype(F32)
                row = lax.broadcasted_iota(jnp.int32, (16, LANES), 0)
                pair = jnp.where(row == 0, high, jnp.where(row == 1, below - high, 0.0))
                sbuf[kk, j, :HD, :] = total.astype(BF16)
                sbuf[kk, j, HD:, :] = pair.astype(BF16)
            for o in range(GROUP - 1):
                part_send(kk, o, peers[o], g).start()

    def finish(kk):
        for o in range(GROUP - 1):
            part_send(kk, o, sources[o], sources[o]).wait_recv()
        total = sbuf[kk, g].astype(F32)
        for o in range(GROUP - 1):
            total = total + rbuf[kk, sources[o]].astype(F32)
        below = total[HD:HD + 1] + total[HD + 1:HD + 2]
        live = jnp.max(mall[g][:MAXT], axis=0, keepdims=True) == 1
        inverse = 1.0 / jnp.where(live, below, 1.0)
        result = jnp.where(live, total[:HD] * inverse, 0.0)
        obuf[kk] = result.T.astype(BF16)

        @pl.when(kk == 1)
        def _():
            out_send().start()

    def body(t, carry):
        @pl.when(t < PER_K)
        def _():
            feat_copy(t).wait()

        for kk in range(KHALF):
            @pl.when(t == kk * PER_K)
            def _():
                for direction in range(2):
                    weight_copy(direction, kk).wait()

        up = t - SKEW * z
        down = t - SKEW * (NZ - 1 - z)
        d = t - LAST

        @pl.when((up >= 0) & (up < STEPS))
        def _():
            add_link(0, up)

        @pl.when((down >= 0) & (down < STEPS))
        def _():
            add_link(1, down)

        @pl.when(is_end & (t == 1))
        def _():
            q_up(0, g).wait_recv()
            for o in range(GROUP - 1):
                q_forward(0, o, g).start()

        @pl.when(is_end & (d == 0))
        def _():
            for o in range(GROUP - 1):
                meta_forward(o, sources[o]).wait_recv()
                for half in range(2):
                    q_forward(half, o, sources[o]).wait_recv()

        @pl.when(is_end & (d >= 0) & (d < STEPS))
        def _():
            attend(d)

        late = d - PER_K - UNIT + 1

        @pl.when(is_end & (late >= 0) & (lax.rem(late + PER_K, PER_K) == 0))
        def _():
            finish(late // PER_K)

        return carry

    lax.fori_loop(0, STEPS + LAST + UNIT, body, 0)

    @pl.when(is_end)
    def _():
        for h in range(2 * KVH):
            out[0, :, h * HD:(h + 1) * HD] = obuf[2 + h // 8, (h % 8) * 64:(h % 8 + 1) * 64, :]
        out_send().wait_send()
        for o in range(GROUP - 1):
            meta_forward(o, g).wait_send()
            for half in range(2):
                q_forward(half, o, g).wait_send()
            for kk in range(KHALF):
                part_send(kk, o, peers[o], g).wait_send()

    @pl.when(jnp.logical_not(is_end))
    def _():
        out_send().wait_recv()
        for h in range(2 * KVH):
            out[0, :, h * HD:(h + 1) * HD] = nbuf[h // 8, (h % 8) * 64:(h % 8 + 1) * 64, :]
        q_up(0, g).wait_send()

    def drain(direction):
        def each(i, carry):
            chain(direction, i).wait_send()
            return carry

        lax.fori_loop(0, STEPS, each, 0)
        for kk in range(KHALF):
            tail_chain(direction, kk).wait_send()

    @pl.when(z < NZ - 1)
    def _():
        drain(0)

    @pl.when(z > 0)
    def _():
        drain(1)


def local(
    tile_features, projection, queries, query_gain, key_gain,
    tile_count, tile_slot, cross_mask, prompt_length,
):
    width = tile_features.shape[2]
    prompt_rows = queries.shape[1]
    whole_rows = UNIT * ROWS
    tail = jnp.pad(tile_features[:, whole_rows, :], ((0, 16 - SLOTS_HERE), (0, 0)))
    weight = projection.transpose(1, 0, 2)
    tiles = jnp.arange(MAXT, dtype=jnp.int32)
    rows = jnp.arange(prompt_rows, dtype=jnp.int32)
    usable = (
        (cross_mask[0].T == 1)
        & (tiles[:, None] < tile_count[0])
        & (rows[None, :] < prompt_length[0])
    ).astype(jnp.int32)
    usable = jnp.tile(usable, (1, HEADS // KVH))
    held = jnp.where(tiles < tile_count[0], tile_slot[0], -1)
    meta = jnp.concatenate([usable, jnp.broadcast_to(held[:, None], (MAXT, LANES))], axis=0)

    vmem = pl.BlockSpec(memory_space=pltpu.VMEM)
    hbm = pl.BlockSpec(memory_space=pl.ANY)
    dma = pltpu.SemaphoreType.DMA
    return pl.pallas_call(
        kernel,
        out_shape=jax.ShapeDtypeStruct(queries.shape, BF16),
        in_specs=[hbm, vmem, hbm, vmem, vmem, vmem, vmem],
        out_specs=vmem,
        scratch_shapes=[
            pltpu.VMEM((SLOTS_HERE, UNIT, ROWS, width), BF16),
            pltpu.VMEM((2, KHALF, width, 2 * HD), BF16),
            pltpu.VMEM((2, STEPS, ROWS, 2 * HD), BF16),
            pltpu.VMEM((2, KHALF, 16, 2 * HD), BF16),
            pltpu.VMEM((GROUP, KHALF, LANES, HD), BF16),
            pltpu.VMEM((GROUP, 2 * MAXT, LANES), jnp.int32),
            pltpu.VMEM((LANES, HD), BF16),
            pltpu.VMEM((HD, LANES), F32),
            pltpu.VMEM((1, LANES), F32),
            pltpu.VMEM((GROUP, HD, LANES), F32),
            pltpu.VMEM((GROUP, 1, LANES), F32),
            pltpu.VMEM((KHALF, GROUP, HD + 16, LANES), BF16),
            pltpu.VMEM((KHALF, GROUP, HD + 16, LANES), BF16),
            pltpu.VMEM((KHALF, LANES, HD), BF16),
            pltpu.VMEM((2, LANES, HD), BF16),
            dma((PER_K,)),
            dma((2, KHALF)),
            dma((2, STEPS)),
            dma((2, STEPS)),
            dma((2, KHALF)),
            dma((2, KHALF)),
            dma,
            dma,
            dma((2, GROUP - 1)),
            dma((2, GROUP - 1)),
            dma((GROUP - 1,)),
            dma((GROUP - 1,)),
            dma((KHALF, GROUP - 1)),
            dma((KHALF, GROUP - 1)),
            dma,
            dma,
        ],
        compiler_params=pltpu.CompilerParams(
            collective_id=0, has_side_effects=True, vmem_limit_bytes=58 * 1024 * 1024
        ),
        cost_estimate=pl.CostEstimate(
            flops=30_000_000_000, bytes_accessed=25_000_000, transcendentals=7_000_000
        ),
    )(
        tile_features, tail, weight, queries,
        query_gain.reshape(1, HD), key_gain.reshape(1, HD), meta,
    )


def solution(mesh):
    in_specs = (
        P("dp", None, "head"),
        P("head", None, None),
        P("dp", None, "head"),
        P(),
        P(),
        P("dp"),
        P("dp", None),
        P("dp", None, None),
        P("dp"),
    )
    out_specs = P("dp", None, "head")
    return jax.shard_map(local, mesh=mesh, in_specs=in_specs, out_specs=out_specs, check_vma=False)
```

```python
import math

import jax
import jax.numpy as jnp
from jax import lax
from jax.experimental import pallas as pl
from jax.experimental.pallas import tpu as pltpu
from jax.sharding import PartitionSpec as P

HEADS = 64
KVH = 8
HD = 128
MAXT = 4
GROUP = 4
NZ = 4
SLOTS_HERE = 2
ROWS = 160
UNIT = 10
LANES = 512
SKEW = 2
LAG = 5
KHALF = KVH // 2
PAIRS = ROWS * SLOTS_HERE
STEPS = KHALF * UNIT
LAST = (NZ - 1) * SKEW
MESH = pl.DeviceIdType.MESH
F32 = jnp.float32
BF16 = jnp.bfloat16


def weight_head(direction, kk):
    return KHALF + kk if direction == 0 else (kk + 2) % KHALF


def kernel(
    feat, weight, query, qgain, kgain, meta, out,
    fraw, traw, fbuf, tail, kvf, wbuf, acc, tacc, qall, mall, qcur, num, den, sbuf, rbuf, obuf, nbuf,
    fsem, xsem, wsem, csend, crecv, tsend, trecv, qzs, qzr, qfs, qfr, ms, mr, ss, sr, os_, or_,
):
    dp = lax.axis_index("dp")
    z = lax.axis_index("head")
    g = lax.rem(dp, GROUP)
    base = dp - g
    is_end = (z == 0) | (z == NZ - 1)
    peers = [lax.rem(g + o, GROUP) for o in range(1, GROUP)]
    sources = [lax.rem(g + GROUP - o, GROUP) for o in range(1, GROUP)]
    beside = jnp.where(z == 0, 1, jnp.where(z == 1, 0, jnp.where(z == 2, 3, 2)))
    final = jnp.where(z == 0, 1, 0)

    def weight_copy(direction, kk):
        return pltpu.make_async_copy(
            weight.at[weight_head(direction, kk)], wbuf.at[direction, kk], wsem.at[direction, kk]
        )

    def feat_copy(i):
        return pltpu.make_async_copy(
            feat.at[pl.ds(i * ROWS, ROWS)], fraw.at[i], fsem.at[i]
        )

    def tail_copy():
        return pltpu.make_async_copy(
            feat.at[pl.ds(UNIT * ROWS, 1)], traw.at[pl.ds(0, 1)], xsem
        )

    for direction in range(2):
        weight_copy(direction, 0).start()
    traw[...] = jnp.zeros_like(traw)
    tail_copy().start()
    for i in range(UNIT):
        feat_copy(i).start()
    for kk in range(1, KHALF):
        for direction in range(2):
            weight_copy(direction, kk).start()

    barrier = pltpu.get_barrier_semaphore()
    for p in peers:
        pl.semaphore_signal(barrier, inc=1, device_id={"dp": base + p}, device_id_type=MESH)

    @pl.when(z > 0)
    def _():
        pl.semaphore_signal(barrier, inc=1, device_id={"head": z - 1}, device_id_type=MESH)

    @pl.when(z < NZ - 1)
    def _():
        pl.semaphore_signal(barrier, inc=1, device_id={"head": z + 1}, device_id_type=MESH)

    for h in range(2 * KVH):
        block = query[0, :, h * HD:(h + 1) * HD].astype(F32)
        squares = jnp.mean(block * block, axis=-1, keepdims=True)
        normed = block * lax.rsqrt(squares + 1e-05) * qgain[...]
        qall[g, 2 + h // 8, (h % 8) * 64:(h % 8 + 1) * 64, :] = normed.astype(BF16)
    mall[g] = meta[...]

    @pl.when(is_end)
    def _():
        pl.semaphore_wait(barrier, GROUP)

    @pl.when(jnp.logical_not(is_end))
    def _():
        pl.semaphore_wait(barrier, GROUP + 1)

    def q_up(dst_half, row):
        return pltpu.make_async_remote_copy(
            src_ref=qall.at[row, pl.ds(2, 2)], dst_ref=qall.at[row, pl.ds(dst_half, 2)],
            send_sem=qzs, recv_sem=qzr, device_id={"head": beside}, device_id_type=MESH,
        )

    def q_forward(half, o, row):
        return pltpu.make_async_remote_copy(
            src_ref=qall.at[row, pl.ds(2 * half, 2)], dst_ref=qall.at[row, pl.ds(2 * half, 2)],
            send_sem=qfs.at[half, o], recv_sem=qfr.at[half, o],
            device_id={"dp": base + peers[o]}, device_id_type=MESH,
        )

    def meta_forward(o, row):
        return pltpu.make_async_remote_copy(
            src_ref=mall.at[row], dst_ref=mall.at[row], send_sem=ms.at[o], recv_sem=mr.at[o],
            device_id={"dp": base + peers[o]}, device_id_type=MESH,
        )

    def part_send(kk, o, src_row, dst_row):
        return pltpu.make_async_remote_copy(
            src_ref=sbuf.at[kk, src_row], dst_ref=rbuf.at[kk, dst_row],
            send_sem=ss.at[kk, o], recv_sem=sr.at[kk, o],
            device_id={"dp": base + peers[o]}, device_id_type=MESH,
        )

    def out_send():
        return pltpu.make_async_remote_copy(
            src_ref=obuf.at[pl.ds(0, 2)], dst_ref=nbuf, send_sem=os_, recv_sem=or_,
            device_id={"head": beside}, device_id_type=MESH,
        )

    @pl.when(jnp.logical_not(is_end))
    def _():
        q_up(0, g).start()

    @pl.when(is_end)
    def _():
        for o in range(GROUP - 1):
            meta_forward(o, g).start()
            q_forward(1, o, g).start()

    def chain(direction, i):
        step = 1 if direction == 0 else -1
        return pltpu.make_async_remote_copy(
            src_ref=acc.at[direction, i], dst_ref=acc.at[direction, i],
            send_sem=csend.at[direction, i], recv_sem=crecv.at[direction, i],
            device_id={"head": z + step}, device_id_type=MESH,
        )

    def tail_chain(direction, kk):
        step = 1 if direction == 0 else -1
        return pltpu.make_async_remote_copy(
            src_ref=tacc.at[direction, kk], dst_ref=tacc.at[direction, kk],
            send_sem=tsend.at[direction, kk], recv_sem=trecv.at[direction, kk],
            device_id={"head": z + step}, device_id_type=MESH,
        )

    def add_link(direction, i):
        first = (z == 0) if direction == 0 else (z == NZ - 1)
        last = (z == NZ - 1) if direction == 0 else (z == 0)
        kk = i // UNIT
        c = lax.rem(i, UNIT)

        @pl.when(lax.rem(i, UNIT) == 0)
        def _():
            part = jnp.dot(tail[...], wbuf[direction, kk], preferred_element_type=F32)

            @pl.when(first)
            def _():
                tacc[direction, kk] = part.astype(BF16)

            @pl.when(jnp.logical_not(first))
            def _():
                tail_chain(direction, kk).wait_recv()
                tacc[direction, kk] = (tacc[direction, kk].astype(F32) + part).astype(BF16)

            @pl.when(jnp.logical_not(last))
            def _():
                tail_chain(direction, kk).start()

        part = jnp.dot(fbuf[c], wbuf[direction, kk], preferred_element_type=F32)

        @pl.when(first)
        def _():
            acc[direction, i] = part.astype(BF16)

        @pl.when(jnp.logical_not(first))
        def _():
            chain(direction, i).wait_recv()
            acc[direction, i] = (acc[direction, i].astype(F32) + part).astype(BF16)

        @pl.when(jnp.logical_not(last))
        def _():
            chain(direction, i).start()

    def weigh(kv, s, valid):
        keys = kv[:, :HD]
        squares = jnp.mean(keys * keys, axis=-1, keepdims=True)
        normed = (keys * lax.rsqrt(squares + 1e-05) * kgain[...]).astype(BF16)
        scores = lax.dot_general(
            normed, qcur[s], (((1,), (1,)), ((), ())), preferred_element_type=F32
        ) * (1.0 / math.sqrt(HD))
        weights = jnp.exp(scores)
        if valid is not None:
            weights = jnp.where(valid, weights, 0.0)
        weights = weights.astype(BF16)
        denominator = jnp.sum(weights.astype(F32), axis=0, keepdims=True)
        numerator = lax.dot_general(
            kv[:, HD:].astype(BF16), weights, (((0,), (0,)), ((), ())), preferred_element_type=F32
        )
        return numerator, denominator

    def hits(j, s):
        rows = mall[j]
        hit = jnp.where(rows[MAXT:2 * MAXT] == dp * SLOTS_HERE + s, 1, 0)
        match = jnp.max(hit, axis=0, keepdims=True)
        usable = jnp.max(hit * rows[:MAXT], axis=0, keepdims=True)
        return match, usable

    def attend(d):
        kk = d // UNIT

        @pl.when(lax.rem(d, UNIT) == 0)
        def _():
            row = lax.broadcasted_iota(jnp.int32, (16, LANES), 0)
            for s in range(SLOTS_HERE):
                chosen = jnp.zeros((LANES, HD), F32)
                for j in range(GROUP):
                    match, _u = hits(j, s)
                    chosen = chosen + match[:, :HD].astype(F32) * qall[j, kk].astype(F32)
                qcur[s] = chosen.astype(BF16)
                n0, d0 = weigh(tacc[final, kk].astype(F32), s, row == s)
                num[s] = n0
                den[s] = d0

        kvf[0] = acc[final, d, :, :HD].astype(F32)
        kvf[1] = acc[final, d, :, HD:].astype(F32)
        for s in range(SLOTS_HERE):
            every = pl.ds(s, ROWS, stride=SLOTS_HERE)
            own = jnp.concatenate([kvf[0, every, :], kvf[1, every, :]], axis=1)
            n1, d1 = weigh(own, s, None)
            num[s] += n1
            den[s] += d1

        @pl.when(lax.rem(d, UNIT) == UNIT - 1)
        def _():
            row = lax.broadcasted_iota(jnp.int32, (16, LANES), 0)
            for j in range(GROUP):
                total = jnp.zeros((HD, LANES), F32)
                below = jnp.zeros((1, LANES), F32)
                for s in range(SLOTS_HERE):
                    _m, usable = hits(j, s)
                    total = total + jnp.where(usable == 1, num[s], 0.0)
                    below = below + jnp.where(usable == 1, den[s], 0.0)
                high = below.astype(BF16).astype(F32)
                pair = jnp.where(row == 0, high, jnp.where(row == 1, below - high, 0.0))
                sbuf[kk, j, :HD, :] = total.astype(BF16)
                sbuf[kk, j, HD:, :] = pair.astype(BF16)
            for o in range(GROUP - 1):
                part_send(kk, o, peers[o], g).start()

    def finish(kk):
        for o in range(GROUP - 1):
            part_send(kk, o, sources[o], sources[o]).wait_recv()
        total = sbuf[kk, g].astype(F32)
        for o in range(GROUP - 1):
            total = total + rbuf[kk, sources[o]].astype(F32)
        below = total[HD:HD + 1] + total[HD + 1:HD + 2]
        live = jnp.max(mall[g][:MAXT], axis=0, keepdims=True) == 1
        inverse = 1.0 / jnp.where(live, below, 1.0)
        result = jnp.where(live, total[:HD] * inverse, 0.0)
        obuf[kk] = result.T.astype(BF16)

        @pl.when(kk == 1)
        def _():
            out_send().start()

    def body(t, carry):
        @pl.when(t < UNIT)
        def _():
            feat_copy(t).wait()
            fbuf[t] = fraw[t].reshape(PAIRS, fraw.shape[-1])

        @pl.when(t == 0)
        def _():
            tail_copy().wait()
            tail[...] = traw[...].reshape(16, traw.shape[-1])

        for kk in range(KHALF):
            @pl.when(t == kk * UNIT)
            def _():
                for direction in range(2):
                    weight_copy(direction, kk).wait()

        up = t - SKEW * z
        down = t - SKEW * (NZ - 1 - z)
        d = t - LAST

        @pl.when((up >= 0) & (up < STEPS))
        def _():
            add_link(0, up)

        @pl.when((down >= 0) & (down < STEPS))
        def _():
            add_link(1, down)

        @pl.when(is_end & (t == 1))
        def _():
            q_up(0, g).wait_recv()
            for o in range(GROUP - 1):
                q_forward(0, o, g).start()

        @pl.when(is_end & (d == 0))
        def _():
            for o in range(GROUP - 1):
                meta_forward(o, sources[o]).wait_recv()
                for half in range(2):
                    q_forward(half, o, sources[o]).wait_recv()

        @pl.when(is_end & (d >= 0) & (d < STEPS))
        def _():
            attend(d)

        late = d - UNIT - LAG + 1

        @pl.when(is_end & (late >= 0) & (lax.rem(late + UNIT, UNIT) == 0))
        def _():
            finish(late // UNIT)

        return carry

    lax.fori_loop(0, STEPS + LAST + LAG, body, 0)

    @pl.when(is_end)
    def _():
        for h in range(2 * KVH):
            out[0, :, h * HD:(h + 1) * HD] = obuf[2 + h // 8, (h % 8) * 64:(h % 8 + 1) * 64, :]
        out_send().wait_send()
        for o in range(GROUP - 1):
            meta_forward(o, g).wait_send()
            for half in range(2):
                q_forward(half, o, g).wait_send()
            for kk in range(KHALF):
                part_send(kk, o, peers[o], g).wait_send()

    @pl.when(jnp.logical_not(is_end))
    def _():
        out_send().wait_recv()
        for h in range(2 * KVH):
            out[0, :, h * HD:(h + 1) * HD] = nbuf[h // 8, (h % 8) * 64:(h % 8 + 1) * 64, :]
        q_up(0, g).wait_send()

    def drain(direction):
        def each(i, carry):
            chain(direction, i).wait_send()
            return carry

        lax.fori_loop(0, STEPS, each, 0)
        for kk in range(KHALF):
            tail_chain(direction, kk).wait_send()

    @pl.when(z < NZ - 1)
    def _():
        drain(0)

    @pl.when(z > 0)
    def _():
        drain(1)


def local(
    tile_features, projection, queries, query_gain, key_gain,
    tile_count, tile_slot, cross_mask, prompt_length,
):
    width = tile_features.shape[2]
    prompt_rows = queries.shape[1]
    weight = projection.transpose(1, 0, 2)
    tiles = jnp.arange(MAXT, dtype=jnp.int32)
    rows = jnp.arange(prompt_rows, dtype=jnp.int32)
    usable = (
        (cross_mask[0].T == 1)
        & (tiles[:, None] < tile_count[0])
        & (rows[None, :] < prompt_length[0])
    ).astype(jnp.int32)
    usable = jnp.tile(usable, (1, HEADS // KVH))
    held = jnp.where(tiles < tile_count[0], tile_slot[0], -1)
    meta = jnp.concatenate([usable, jnp.broadcast_to(held[:, None], (MAXT, LANES))], axis=0)

    vmem = pl.BlockSpec(memory_space=pltpu.VMEM)
    hbm = pl.BlockSpec(memory_space=pl.ANY)
    dma = pltpu.SemaphoreType.DMA
    return pl.pallas_call(
        kernel,
        out_shape=jax.ShapeDtypeStruct(queries.shape, BF16),
        in_specs=[hbm, hbm, vmem, vmem, vmem, vmem],
        out_specs=vmem,
        scratch_shapes=[
            pltpu.VMEM((UNIT, ROWS, SLOTS_HERE, width), BF16),
            pltpu.VMEM((8, SLOTS_HERE, width), BF16),
            pltpu.VMEM((UNIT, PAIRS, width), BF16),
            pltpu.VMEM((16, width), BF16),
            pltpu.VMEM((2, PAIRS, HD), F32),
            pltpu.VMEM((2, KHALF, width, 2 * HD), BF16),
            pltpu.VMEM((2, STEPS, PAIRS, 2 * HD), BF16),
            pltpu.VMEM((2, KHALF, 16, 2 * HD), BF16),
            pltpu.VMEM((GROUP, KHALF, LANES, HD), BF16),
            pltpu.VMEM((GROUP, 2 * MAXT, LANES), jnp.int32),
            pltpu.VMEM((SLOTS_HERE, LANES, HD), BF16),
            pltpu.VMEM((SLOTS_HERE, HD, LANES), F32),
            pltpu.VMEM((SLOTS_HERE, 1, LANES), F32),
            pltpu.VMEM((KHALF, GROUP, HD + 16, LANES), BF16),
            pltpu.VMEM((KHALF, GROUP, HD + 16, LANES), BF16),
            pltpu.VMEM((KHALF, LANES, HD), BF16),
            pltpu.VMEM((2, LANES, HD), BF16),
            dma((UNIT,)),
            dma,
            dma((2, KHALF)),
            dma((2, STEPS)),
            dma((2, STEPS)),
            dma((2, KHALF)),
            dma((2, KHALF)),
            dma,
            dma,
            dma((2, GROUP - 1)),
            dma((2, GROUP - 1)),
            dma((GROUP - 1,)),
            dma((GROUP - 1,)),
            dma((KHALF, GROUP - 1)),
            dma((KHALF, GROUP - 1)),
            dma,
            dma,
        ],
        compiler_params=pltpu.CompilerParams(
            collective_id=0, has_side_effects=True, vmem_limit_bytes=58 * 1024 * 1024
        ),
        cost_estimate=pl.CostEstimate(
            flops=30_000_000_000, bytes_accessed=25_000_000, transcendentals=7_000_000
        ),
    )(
        tile_features.transpose(1, 0, 2), weight, queries,
        query_gain.reshape(1, HD), key_gain.reshape(1, HD), meta,
    )


def solution(mesh):
    in_specs = (
        P("dp", None, "head"),
        P("head", None, None),
        P("dp", None, "head"),
        P(),
        P(),
        P("dp"),
        P("dp", None),
        P("dp", None, None),
        P("dp"),
    )
    out_specs = P("dp", None, "head")
    return jax.shard_map(local, mesh=mesh, in_specs=in_specs, out_specs=out_specs, check_vma=False)
```

```python
import math

import jax
import jax.numpy as jnp
from jax import lax
from jax.experimental import pallas as pl
from jax.experimental.pallas import tpu as pltpu
from jax.sharding import PartitionSpec as P

HEADS = 64
KVH = 8
HD = 128
MAXT = 4
GROUP = 4
NZ = 4
SLOTS_HERE = 2
ROWS = 160
UNIT = 10
LANES = 512
AHEAD = 3
HALVES = 2
LAG = 5
KHALF = KVH // 2
PAIRS = ROWS * SLOTS_HERE
PIECE = PAIRS // HALVES
STEPS = KHALF * UNIT
LAST = NZ - 1 + AHEAD
MESH = pl.DeviceIdType.MESH
F32 = jnp.float32
BF16 = jnp.bfloat16


def weight_head(direction, kk):
    return jnp.where(direction == 0, KHALF + kk, (kk + 2) % KHALF)


def kernel(
    count, slots, length, feat, weight, query, qgain, kgain, mask, out,
    fraw, traw, fbuf, tail, kvf, wbuf, acc, tacc, qall, mall, qcur, num, den, sbuf, rbuf, obuf, nbuf,
    fsem, xsem, wsem, csend, crecv, tsend, trecv, qzs, qzr, qfs, qfr, ms, mr, ss, sr, os_, or_,
):
    dp = lax.axis_index("dp")
    z = lax.axis_index("head")
    g = lax.rem(dp, GROUP)
    base = dp - g
    is_end = (z == 0) | (z == NZ - 1)
    peers = [lax.rem(g + o, GROUP) for o in range(1, GROUP)]
    sources = [lax.rem(g + GROUP - o, GROUP) for o in range(1, GROUP)]
    beside = jnp.where(z == 0, 1, jnp.where(z == 1, 0, jnp.where(z == 2, 3, 2)))
    final = jnp.where(z == 0, 1, 0)

    def weight_copy(direction, kk):
        return pltpu.make_async_copy(
            weight.at[weight_head(direction, kk)], wbuf.at[direction, kk], wsem.at[direction, kk]
        )

    def feat_copy(i):
        return pltpu.make_async_copy(
            feat.at[pl.ds(i * ROWS, ROWS)], fraw.at[i], fsem.at[i]
        )

    def tail_copy():
        return pltpu.make_async_copy(
            feat.at[pl.ds(UNIT * ROWS, 1)], traw.at[pl.ds(0, 1)], xsem
        )

    near = jnp.where(z < NZ // 2, 0, 1)
    weight_copy(near, 0).start()
    traw[...] = jnp.zeros_like(traw)
    tail_copy().start()
    feat_copy(0).start()
    weight_copy(1 - near, 0).start()

    barrier = pltpu.get_barrier_semaphore()
    for p in peers:
        pl.semaphore_signal(barrier, inc=1, device_id={"dp": base + p}, device_id_type=MESH)

    @pl.when(z > 0)
    def _():
        pl.semaphore_signal(barrier, inc=1, device_id={"head": z - 1}, device_id_type=MESH)

    @pl.when(z < NZ - 1)
    def _():
        pl.semaphore_signal(barrier, inc=1, device_id={"head": z + 1}, device_id_type=MESH)

    tile = lax.broadcasted_iota(jnp.int32, (MAXT, LANES), 0)
    prompt = lax.rem(lax.broadcasted_iota(jnp.int32, (MAXT, LANES), 1), 64)
    seen = jnp.concatenate([mask[0]] * (LANES // 64), axis=1)
    used = (seen == 1) & (tile < count[0]) & (prompt < length[0])
    held = jnp.full((MAXT, LANES), -1, jnp.int32)
    for i in range(MAXT):
        held = jnp.where((tile == i) & (tile < count[0]), slots[0, i], held)
    mall[g, :MAXT] = jnp.where(used, 1, 0)
    mall[g, MAXT:] = held

    @pl.when(is_end)
    def _():
        pl.semaphore_wait(barrier, GROUP)

    @pl.when(jnp.logical_not(is_end))
    def _():
        pl.semaphore_wait(barrier, GROUP + 1)

    def q_up(dst_half, row):
        return pltpu.make_async_remote_copy(
            src_ref=qall.at[row, pl.ds(2, 2)], dst_ref=qall.at[row, pl.ds(dst_half, 2)],
            send_sem=qzs, recv_sem=qzr, device_id={"head": beside}, device_id_type=MESH,
        )

    def q_forward(half, o, row):
        return pltpu.make_async_remote_copy(
            src_ref=qall.at[row, pl.ds(2 * half, 2)], dst_ref=qall.at[row, pl.ds(2 * half, 2)],
            send_sem=qfs.at[half, o], recv_sem=qfr.at[half, o],
            device_id={"dp": base + peers[o]}, device_id_type=MESH,
        )

    def meta_forward(o, row):
        return pltpu.make_async_remote_copy(
            src_ref=mall.at[row], dst_ref=mall.at[row], send_sem=ms.at[o], recv_sem=mr.at[o],
            device_id={"dp": base + peers[o]}, device_id_type=MESH,
        )

    def part_send(kk, o, src_row, dst_row):
        return pltpu.make_async_remote_copy(
            src_ref=sbuf.at[kk, src_row], dst_ref=rbuf.at[kk, dst_row],
            send_sem=ss.at[kk, o], recv_sem=sr.at[kk, o],
            device_id={"dp": base + peers[o]}, device_id_type=MESH,
        )

    def out_send():
        return pltpu.make_async_remote_copy(
            src_ref=obuf.at[pl.ds(0, 2)], dst_ref=nbuf, send_sem=os_, recv_sem=or_,
            device_id={"head": beside}, device_id_type=MESH,
        )

    for i in range(1, UNIT):
        feat_copy(i).start()
    for kk in range(1, KHALF):
        for direction in range(2):
            weight_copy(direction, kk).start()

    def send_queries():
        for h in range(2 * KVH):
            block = query[0, :, h * HD:(h + 1) * HD].astype(F32)
            squares = jnp.mean(block * block, axis=-1, keepdims=True)
            normed = block * lax.rsqrt(squares + 1e-05) * qgain[...]
            qall[g, 2 + h // 8, (h % 8) * 64:(h % 8 + 1) * 64, :] = normed.astype(BF16)

        @pl.when(jnp.logical_not(is_end))
        def _():
            q_up(0, g).start()

        @pl.when(is_end)
        def _():
            for o in range(GROUP - 1):
                meta_forward(o, g).start()
                q_forward(1, o, g).start()

    def chain(direction, i, half):
        step = jnp.where(direction == 0, 1, -1)
        rows = pl.ds(half * PIECE, PIECE)
        return pltpu.make_async_remote_copy(
            src_ref=acc.at[direction, i, rows], dst_ref=acc.at[direction, i, rows],
            send_sem=csend.at[direction, half, i], recv_sem=crecv.at[direction, half, i],
            device_id={"head": z + step}, device_id_type=MESH,
        )

    def tail_chain(direction, kk):
        step = jnp.where(direction == 0, 1, -1)
        return pltpu.make_async_remote_copy(
            src_ref=tacc.at[direction, kk], dst_ref=tacc.at[direction, kk],
            send_sem=tsend.at[direction, kk], recv_sem=trecv.at[direction, kk],
            device_id={"head": z + step}, device_id_type=MESH,
        )

    def add_link(direction, i):
        first = z == jnp.where(direction == 0, 0, NZ - 1)
        last = z == jnp.where(direction == 0, NZ - 1, 0)
        kk = i // UNIT
        c = lax.rem(i, UNIT)

        @pl.when(lax.rem(i, UNIT) == 0)
        def _():
            part = jnp.dot(tail[...], wbuf[direction, kk], preferred_element_type=F32)

            @pl.when(first)
            def _():
                tacc[direction, kk] = part.astype(BF16)

            @pl.when(jnp.logical_not(first))
            def _():
                tail_chain(direction, kk).wait_recv()
                tacc[direction, kk] = (tacc[direction, kk].astype(F32) + part).astype(BF16)

            @pl.when(jnp.logical_not(last))
            def _():
                tail_chain(direction, kk).start()

        part = jnp.dot(fbuf[c], wbuf[direction, kk], preferred_element_type=F32)

        for half in range(HALVES):
            rows = slice(half * PIECE, (half + 1) * PIECE)

            @pl.when(first)
            def _():
                acc[direction, i, rows] = part[rows].astype(BF16)

            @pl.when(jnp.logical_not(first))
            def _():
                chain(direction, i, half).wait_recv()
                held_sum = acc[direction, i, rows].astype(F32)
                acc[direction, i, rows] = (held_sum + part[rows]).astype(BF16)

            @pl.when(jnp.logical_not(last))
            def _():
                chain(direction, i, half).start()

    def weigh(kv, s, valid):
        keys = kv[:, :HD]
        squares = jnp.mean(keys * keys, axis=-1, keepdims=True)
        normed = (keys * lax.rsqrt(squares + 1e-05) * kgain[...]).astype(BF16)
        scores = lax.dot_general(
            normed, qcur[s], (((1,), (1,)), ((), ())), preferred_element_type=F32
        ) * (1.0 / math.sqrt(HD))
        weights = jnp.exp(scores)
        if valid is not None:
            weights = jnp.where(valid, weights, 0.0)
        weights = weights.astype(BF16)
        denominator = jnp.sum(weights.astype(F32), axis=0, keepdims=True)
        numerator = lax.dot_general(
            kv[:, HD:].astype(BF16), weights, (((0,), (0,)), ((), ())), preferred_element_type=F32
        )
        return numerator, denominator

    def hits(j, s):
        rows = mall[j]
        hit = jnp.where(rows[MAXT:2 * MAXT] == dp * SLOTS_HERE + s, 1, 0)
        match = jnp.max(hit, axis=0, keepdims=True)
        usable = jnp.max(hit * rows[:MAXT], axis=0, keepdims=True)
        return match, usable

    def attend(d):
        kk = d // UNIT

        @pl.when(lax.rem(d, UNIT) == 0)
        def _():
            row = lax.broadcasted_iota(jnp.int32, (16, LANES), 0)
            for s in range(SLOTS_HERE):
                chosen = jnp.zeros((LANES, HD), F32)
                for j in range(GROUP):
                    match, _u = hits(j, s)
                    chosen = chosen + match[:, :HD].astype(F32) * qall[j, kk].astype(F32)
                qcur[s] = chosen.astype(BF16)
                n0, d0 = weigh(tacc[final, kk].astype(F32), s, row == s)
                num[s] = n0
                den[s] = d0

        kvf[0] = acc[final, d, :, :HD].astype(F32)
        kvf[1] = acc[final, d, :, HD:].astype(F32)
        for s in range(SLOTS_HERE):
            every = pl.ds(s, ROWS, stride=SLOTS_HERE)
            own = jnp.concatenate([kvf[0, every, :], kvf[1, every, :]], axis=1)
            n1, d1 = weigh(own, s, None)
            num[s] += n1
            den[s] += d1

        @pl.when(lax.rem(d, UNIT) == UNIT - 1)
        def _():
            row = lax.broadcasted_iota(jnp.int32, (16, LANES), 0)
            for j in range(GROUP):
                total = jnp.zeros((HD, LANES), F32)
                below = jnp.zeros((1, LANES), F32)
                for s in range(SLOTS_HERE):
                    _m, usable = hits(j, s)
                    total = total + jnp.where(usable == 1, num[s], 0.0)
                    below = below + jnp.where(usable == 1, den[s], 0.0)
                high = below.astype(BF16).astype(F32)
                pair = jnp.where(row == 0, high, jnp.where(row == 1, below - high, 0.0))
                sbuf[kk, j, :HD, :] = total.astype(BF16)
                sbuf[kk, j, HD:, :] = pair.astype(BF16)
            for o in range(GROUP - 1):
                part_send(kk, o, peers[o], g).start()

    def finish(kk):
        for o in range(GROUP - 1):
            part_send(kk, o, sources[o], sources[o]).wait_recv()
        total = sbuf[kk, g].astype(F32)
        for o in range(GROUP - 1):
            total = total + rbuf[kk, sources[o]].astype(F32)
        below = total[HD:HD + 1] + total[HD + 1:HD + 2]
        live = jnp.max(mall[g][:MAXT], axis=0, keepdims=True) == 1
        inverse = 1.0 / jnp.where(live, below, 1.0)
        result = jnp.where(live, total[:HD] * inverse, 0.0)
        obuf[kk] = result.T.astype(BF16)

        @pl.when(kk == 1)
        def _():
            out_send().start()

    def body(t, carry):
        @pl.when(t < UNIT)
        def _():
            feat_copy(t).wait()
            fbuf[t] = fraw[t].reshape(PAIRS, fraw.shape[-1])

        @pl.when(t == 0)
        def _():
            tail_copy().wait()
            tail[...] = traw[...].reshape(16, traw.shape[-1])

        for kk in range(KHALF):
            @pl.when(t == kk * UNIT)
            def _():
                for direction in range(2):
                    weight_copy(direction, kk).wait()

        near_hop = jnp.where(is_end, 0, 1)
        first_i = t - jnp.where(is_end, 0, AHEAD + 1)
        other_i = t - (AHEAD + NZ - 1 - near_hop)
        d = t - LAST

        @pl.when((first_i >= 0) & (first_i < STEPS))
        def _():
            add_link(near, first_i)

        @pl.when((other_i >= 0) & (other_i < STEPS))
        def _():
            add_link(1 - near, other_i)

        @pl.when(t == 1)
        def _():
            send_queries()

        @pl.when(is_end & (t == 3))
        def _():
            q_up(0, g).wait_recv()
            for o in range(GROUP - 1):
                q_forward(0, o, g).start()

        @pl.when(is_end & (d == 0))
        def _():
            for o in range(GROUP - 1):
                meta_forward(o, sources[o]).wait_recv()
                for half in range(2):
                    q_forward(half, o, sources[o]).wait_recv()

        @pl.when(is_end & (d >= 0) & (d < STEPS))
        def _():
            attend(d)

        late = d - UNIT - LAG + 1

        @pl.when(is_end & (late >= 0) & (lax.rem(late + UNIT, UNIT) == 0))
        def _():
            finish(late // UNIT)

        return carry

    lax.fori_loop(0, STEPS + LAST + LAG, body, 0)

    @pl.when(is_end)
    def _():
        for h in range(2 * KVH):
            out[0, :, h * HD:(h + 1) * HD] = obuf[2 + h // 8, (h % 8) * 64:(h % 8 + 1) * 64, :]
        out_send().wait_send()
        for o in range(GROUP - 1):
            meta_forward(o, g).wait_send()
            for half in range(2):
                q_forward(half, o, g).wait_send()
            for kk in range(KHALF):
                part_send(kk, o, peers[o], g).wait_send()

    @pl.when(jnp.logical_not(is_end))
    def _():
        out_send().wait_recv()
        for h in range(2 * KVH):
            out[0, :, h * HD:(h + 1) * HD] = nbuf[h // 8, (h % 8) * 64:(h % 8 + 1) * 64, :]
        q_up(0, g).wait_send()

    def drain(direction):
        def each(i, carry):
            for half in range(HALVES):
                chain(direction, i, half).wait_send()
            return carry

        lax.fori_loop(0, STEPS, each, 0)
        for kk in range(KHALF):
            tail_chain(direction, kk).wait_send()

    @pl.when(z < NZ - 1)
    def _():
        drain(0)

    @pl.when(z > 0)
    def _():
        drain(1)


def local(
    tile_features, projection, queries, query_gain, key_gain,
    tile_count, tile_slot, cross_mask, prompt_length,
):
    width = tile_features.shape[2]
    weight = projection.transpose(1, 0, 2)
    mask = cross_mask.transpose(0, 2, 1)

    vmem = pl.BlockSpec(memory_space=pltpu.VMEM)
    hbm = pl.BlockSpec(memory_space=pl.ANY)
    smem = pl.BlockSpec(memory_space=pltpu.SMEM)
    dma = pltpu.SemaphoreType.DMA
    return pl.pallas_call(
        kernel,
        out_shape=jax.ShapeDtypeStruct(queries.shape, BF16),
        in_specs=[smem, smem, smem, hbm, hbm, vmem, vmem, vmem, vmem],
        out_specs=vmem,
        scratch_shapes=[
            pltpu.VMEM((UNIT, ROWS, SLOTS_HERE, width), BF16),
            pltpu.VMEM((8, SLOTS_HERE, width), BF16),
            pltpu.VMEM((UNIT, PAIRS, width), BF16),
            pltpu.VMEM((16, width), BF16),
            pltpu.VMEM((2, PAIRS, HD), F32),
            pltpu.VMEM((2, KHALF, width, 2 * HD), BF16),
            pltpu.VMEM((2, STEPS, PAIRS, 2 * HD), BF16),
            pltpu.VMEM((2, KHALF, 16, 2 * HD), BF16),
            pltpu.VMEM((GROUP, KHALF, LANES, HD), BF16),
            pltpu.VMEM((GROUP, 2 * MAXT, LANES), jnp.int32),
            pltpu.VMEM((SLOTS_HERE, LANES, HD), BF16),
            pltpu.VMEM((SLOTS_HERE, HD, LANES), F32),
            pltpu.VMEM((SLOTS_HERE, 1, LANES), F32),
            pltpu.VMEM((KHALF, GROUP, HD + 16, LANES), BF16),
            pltpu.VMEM((KHALF, GROUP, HD + 16, LANES), BF16),
            pltpu.VMEM((KHALF, LANES, HD), BF16),
            pltpu.VMEM((2, LANES, HD), BF16),
            dma((UNIT,)),
            dma,
            dma((2, KHALF)),
            dma((2, HALVES, STEPS)),
            dma((2, HALVES, STEPS)),
            dma((2, KHALF)),
            dma((2, KHALF)),
            dma,
            dma,
            dma((2, GROUP - 1)),
            dma((2, GROUP - 1)),
            dma((GROUP - 1,)),
            dma((GROUP - 1,)),
            dma((KHALF, GROUP - 1)),
            dma((KHALF, GROUP - 1)),
            dma,
            dma,
        ],
        compiler_params=pltpu.CompilerParams(
            collective_id=0, has_side_effects=True, vmem_limit_bytes=58 * 1024 * 1024
        ),
        cost_estimate=pl.CostEstimate(
            flops=30_000_000_000, bytes_accessed=25_000_000, transcendentals=7_000_000
        ),
    )(
        tile_count, tile_slot, prompt_length, tile_features.transpose(1, 0, 2), weight, queries,
        query_gain.reshape(1, HD), key_gain.reshape(1, HD), mask,
    )


def solution(mesh):
    in_specs = (
        P("dp", None, "head"),
        P("head", None, None),
        P("dp", None, "head"),
        P(),
        P(),
        P("dp"),
        P("dp", None),
        P("dp", None, None),
        P("dp"),
    )
    out_specs = P("dp", None, "head")
    return jax.shard_map(local, mesh=mesh, in_specs=in_specs, out_specs=out_specs, check_vma=False)
```

```python
import math

import jax
import jax.numpy as jnp
from jax import lax
from jax.experimental import pallas as pl
from jax.experimental.pallas import tpu as pltpu
from jax.sharding import PartitionSpec as P

HEADS = 64
KVH = 8
HD = 128
MAXT = 4
GROUP = 4
NZ = 4
SLOTS_HERE = 2
ROWS = 160
UNIT = 10
LANES = 512
AHEAD = 3
HALVES = 4
LAG = 5
KHALF = KVH // 2
PAIRS = ROWS * SLOTS_HERE
PIECE = PAIRS // HALVES
STEPS = KHALF * UNIT
LAST = NZ - 1 + AHEAD
MESH = pl.DeviceIdType.MESH
F32 = jnp.float32
BF16 = jnp.bfloat16


def weight_head(direction, kk):
    return jnp.where(direction == 0, KHALF + kk, (kk + 2) % KHALF)


def kernel(
    count, slots, length, feat, weight, query, qgain, kgain, mask, out,
    fraw, traw, fbuf, tail, kvf, wbuf, acc, tacc, qall, mall, qcur, num, den, sbuf, rbuf, obuf, nbuf,
    fsem, xsem, wsem, csend, crecv, tsend, trecv, qzs, qzr, qfs, qfr, ms, mr, ss, sr, os_, or_,
):
    dp = lax.axis_index("dp")
    z = lax.axis_index("head")
    g = lax.rem(dp, GROUP)
    base = dp - g
    is_end = (z == 0) | (z == NZ - 1)
    peers = [lax.rem(g + o, GROUP) for o in range(1, GROUP)]
    sources = [lax.rem(g + GROUP - o, GROUP) for o in range(1, GROUP)]
    beside = jnp.where(z == 0, 1, jnp.where(z == 1, 0, jnp.where(z == 2, 3, 2)))
    final = jnp.where(z == 0, 1, 0)

    def weight_copy(direction, kk):
        return pltpu.make_async_copy(
            weight.at[weight_head(direction, kk)], wbuf.at[direction, kk], wsem.at[direction, kk]
        )

    def feat_copy(i):
        return pltpu.make_async_copy(
            feat.at[pl.ds(i * ROWS, ROWS)], fraw.at[i], fsem.at[i]
        )

    def tail_copy():
        return pltpu.make_async_copy(
            feat.at[pl.ds(UNIT * ROWS, 1)], traw.at[pl.ds(0, 1)], xsem
        )

    near = jnp.where(z < NZ // 2, 0, 1)
    weight_copy(near, 0).start()
    traw[...] = jnp.zeros_like(traw)
    tail_copy().start()
    feat_copy(0).start()
    weight_copy(1 - near, 0).start()

    barrier = pltpu.get_barrier_semaphore()
    for p in peers:
        pl.semaphore_signal(barrier, inc=1, device_id={"dp": base + p}, device_id_type=MESH)

    @pl.when(z > 0)
    def _():
        pl.semaphore_signal(barrier, inc=1, device_id={"head": z - 1}, device_id_type=MESH)

    @pl.when(z < NZ - 1)
    def _():
        pl.semaphore_signal(barrier, inc=1, device_id={"head": z + 1}, device_id_type=MESH)

    tile = lax.broadcasted_iota(jnp.int32, (MAXT, LANES), 0)
    prompt = lax.rem(lax.broadcasted_iota(jnp.int32, (MAXT, LANES), 1), 64)
    seen = jnp.concatenate([mask[0]] * (LANES // 64), axis=1)
    used = (seen == 1) & (tile < count[0]) & (prompt < length[0])
    held = jnp.full((MAXT, LANES), -1, jnp.int32)
    for i in range(MAXT):
        held = jnp.where((tile == i) & (tile < count[0]), slots[0, i], held)
    mall[g, :MAXT] = jnp.where(used, 1, 0)
    mall[g, MAXT:] = held

    @pl.when(is_end)
    def _():
        pl.semaphore_wait(barrier, GROUP)

    @pl.when(jnp.logical_not(is_end))
    def _():
        pl.semaphore_wait(barrier, GROUP + 1)

    def q_up(dst_half, row):
        return pltpu.make_async_remote_copy(
            src_ref=qall.at[row, pl.ds(2, 2)], dst_ref=qall.at[row, pl.ds(dst_half, 2)],
            send_sem=qzs, recv_sem=qzr, device_id={"head": beside}, device_id_type=MESH,
        )

    def q_forward(half, o, row):
        return pltpu.make_async_remote_copy(
            src_ref=qall.at[row, pl.ds(2 * half, 2)], dst_ref=qall.at[row, pl.ds(2 * half, 2)],
            send_sem=qfs.at[half, o], recv_sem=qfr.at[half, o],
            device_id={"dp": base + peers[o]}, device_id_type=MESH,
        )

    def meta_forward(o, row):
        return pltpu.make_async_remote_copy(
            src_ref=mall.at[row], dst_ref=mall.at[row], send_sem=ms.at[o], recv_sem=mr.at[o],
            device_id={"dp": base + peers[o]}, device_id_type=MESH,
        )

    def part_send(kk, o, src_row, dst_row):
        return pltpu.make_async_remote_copy(
            src_ref=sbuf.at[kk, src_row], dst_ref=rbuf.at[kk, dst_row],
            send_sem=ss.at[kk, o], recv_sem=sr.at[kk, o],
            device_id={"dp": base + peers[o]}, device_id_type=MESH,
        )

    def out_send():
        return pltpu.make_async_remote_copy(
            src_ref=obuf.at[pl.ds(0, 2)], dst_ref=nbuf, send_sem=os_, recv_sem=or_,
            device_id={"head": beside}, device_id_type=MESH,
        )

    for i in range(1, UNIT):
        feat_copy(i).start()
    for kk in range(1, KHALF):
        for direction in range(2):
            weight_copy(direction, kk).start()

    def send_queries():
        for h in range(2 * KVH):
            block = query[0, :, h * HD:(h + 1) * HD].astype(F32)
            squares = jnp.mean(block * block, axis=-1, keepdims=True)
            normed = block * lax.rsqrt(squares + 1e-05) * qgain[...]
            qall[g, 2 + h // 8, (h % 8) * 64:(h % 8 + 1) * 64, :] = normed.astype(BF16)

        @pl.when(jnp.logical_not(is_end))
        def _():
            q_up(0, g).start()

        @pl.when(is_end)
        def _():
            for o in range(GROUP - 1):
                meta_forward(o, g).start()
                q_forward(1, o, g).start()

    def chain(direction, i, half):
        step = jnp.where(direction == 0, 1, -1)
        rows = pl.ds(half * PIECE, PIECE)
        return pltpu.make_async_remote_copy(
            src_ref=acc.at[direction, i, rows], dst_ref=acc.at[direction, i, rows],
            send_sem=csend.at[direction, half, i], recv_sem=crecv.at[direction, half, i],
            device_id={"head": z + step}, device_id_type=MESH,
        )

    def tail_chain(direction, kk):
        step = jnp.where(direction == 0, 1, -1)
        return pltpu.make_async_remote_copy(
            src_ref=tacc.at[direction, kk], dst_ref=tacc.at[direction, kk],
            send_sem=tsend.at[direction, kk], recv_sem=trecv.at[direction, kk],
            device_id={"head": z + step}, device_id_type=MESH,
        )

    def add_link(direction, i):
        first = z == jnp.where(direction == 0, 0, NZ - 1)
        last = z == jnp.where(direction == 0, NZ - 1, 0)
        kk = i // UNIT
        c = lax.rem(i, UNIT)

        part = jnp.dot(fbuf[c], wbuf[direction, kk], preferred_element_type=F32)

        for half in range(HALVES):
            rows = slice(half * PIECE, (half + 1) * PIECE)

            @pl.when(first)
            def _():
                acc[direction, i, rows] = part[rows].astype(BF16)

            @pl.when(jnp.logical_not(first))
            def _():
                chain(direction, i, half).wait_recv()
                held_sum = acc[direction, i, rows].astype(F32)
                acc[direction, i, rows] = (held_sum + part[rows]).astype(BF16)

            @pl.when(jnp.logical_not(last))
            def _():
                chain(direction, i, half).start()

        @pl.when(lax.rem(i, UNIT) == 0)
        def _():
            part = jnp.dot(tail[...], wbuf[direction, kk], preferred_element_type=F32)

            @pl.when(first)
            def _():
                tacc[direction, kk] = part.astype(BF16)

            @pl.when(jnp.logical_not(first))
            def _():
                tail_chain(direction, kk).wait_recv()
                tacc[direction, kk] = (tacc[direction, kk].astype(F32) + part).astype(BF16)

            @pl.when(jnp.logical_not(last))
            def _():
                tail_chain(direction, kk).start()

    def weigh(kv, s, valid):
        keys = kv[:, :HD]
        squares = jnp.mean(keys * keys, axis=-1, keepdims=True)
        normed = (keys * lax.rsqrt(squares + 1e-05) * kgain[...]).astype(BF16)
        scores = lax.dot_general(
            normed, qcur[s], (((1,), (1,)), ((), ())), preferred_element_type=F32
        ) * (1.0 / math.sqrt(HD))
        weights = jnp.exp(scores)
        if valid is not None:
            weights = jnp.where(valid, weights, 0.0)
        weights = weights.astype(BF16)
        denominator = jnp.sum(weights.astype(F32), axis=0, keepdims=True)
        numerator = lax.dot_general(
            kv[:, HD:].astype(BF16), weights, (((0,), (0,)), ((), ())), preferred_element_type=F32
        )
        return numerator, denominator

    def hits(j, s):
        rows = mall[j]
        hit = jnp.where(rows[MAXT:2 * MAXT] == dp * SLOTS_HERE + s, 1, 0)
        match = jnp.max(hit, axis=0, keepdims=True)
        usable = jnp.max(hit * rows[:MAXT], axis=0, keepdims=True)
        return match, usable

    def attend(d):
        kk = d // UNIT

        @pl.when(lax.rem(d, UNIT) == 0)
        def _():
            row = lax.broadcasted_iota(jnp.int32, (16, LANES), 0)
            for s in range(SLOTS_HERE):
                chosen = jnp.zeros((LANES, HD), F32)
                for j in range(GROUP):
                    match, _u = hits(j, s)
                    chosen = chosen + match[:, :HD].astype(F32) * qall[j, kk].astype(F32)
                qcur[s] = chosen.astype(BF16)
                n0, d0 = weigh(tacc[final, kk].astype(F32), s, row == s)
                num[s] = n0
                den[s] = d0

        kvf[0] = acc[final, d, :, :HD].astype(F32)
        kvf[1] = acc[final, d, :, HD:].astype(F32)
        for s in range(SLOTS_HERE):
            every = pl.ds(s, ROWS, stride=SLOTS_HERE)
            own = jnp.concatenate([kvf[0, every, :], kvf[1, every, :]], axis=1)
            n1, d1 = weigh(own, s, None)
            num[s] += n1
            den[s] += d1

        @pl.when(lax.rem(d, UNIT) == UNIT - 1)
        def _():
            row = lax.broadcasted_iota(jnp.int32, (16, LANES), 0)
            for o in (1, 0, 2, None):
                j = g if o is None else peers[o]
                total = jnp.zeros((HD, LANES), F32)
                below = jnp.zeros((1, LANES), F32)
                for s in range(SLOTS_HERE):
                    _m, usable = hits(j, s)
                    total = total + jnp.where(usable == 1, num[s], 0.0)
                    below = below + jnp.where(usable == 1, den[s], 0.0)
                high = below.astype(BF16).astype(F32)
                pair = jnp.where(row == 0, high, jnp.where(row == 1, below - high, 0.0))
                sbuf[kk, j, :HD, :] = total.astype(BF16)
                sbuf[kk, j, HD:, :] = pair.astype(BF16)
                if o is not None:
                    part_send(kk, o, j, g).start()

    def finish(kk):
        for o in range(GROUP - 1):
            part_send(kk, o, sources[o], sources[o]).wait_recv()
        total = sbuf[kk, g].astype(F32)
        for o in range(GROUP - 1):
            total = total + rbuf[kk, sources[o]].astype(F32)
        below = total[HD:HD + 1] + total[HD + 1:HD + 2]
        live = jnp.max(mall[g][:MAXT], axis=0, keepdims=True) == 1
        inverse = 1.0 / jnp.where(live, below, 1.0)
        result = jnp.where(live, total[:HD] * inverse, 0.0)
        obuf[kk] = result.T.astype(BF16)

        @pl.when(kk == 1)
        def _():
            out_send().start()

    def body(t, carry):
        @pl.when(t < UNIT)
        def _():
            feat_copy(t).wait()
            fbuf[t] = fraw[t].reshape(PAIRS, fraw.shape[-1])

        @pl.when(t == 0)
        def _():
            tail_copy().wait()
            tail[...] = traw[...].reshape(16, traw.shape[-1])

        for kk in range(KHALF):
            @pl.when(t == kk * UNIT)
            def _():
                for direction in range(2):
                    weight_copy(direction, kk).wait()

        near_hop = jnp.where(is_end, 0, 1)
        first_i = t - jnp.where(is_end, 0, AHEAD + 1)
        other_i = t - (AHEAD + NZ - 1 - near_hop)
        d = t - LAST

        @pl.when((first_i >= 0) & (first_i < STEPS))
        def _():
            add_link(near, first_i)

        @pl.when((other_i >= 0) & (other_i < STEPS))
        def _():
            add_link(1 - near, other_i)

        @pl.when(t == 1)
        def _():
            send_queries()

        @pl.when(is_end & (t == 3))
        def _():
            q_up(0, g).wait_recv()
            for o in range(GROUP - 1):
                q_forward(0, o, g).start()

        @pl.when(is_end & (d == 0))
        def _():
            for o in range(GROUP - 1):
                meta_forward(o, sources[o]).wait_recv()
                for half in range(2):
                    q_forward(half, o, sources[o]).wait_recv()

        @pl.when(is_end & (d >= 0) & (d < STEPS))
        def _():
            attend(d)

        late = d - UNIT - LAG + 1

        @pl.when(is_end & (late >= 0) & (lax.rem(late + UNIT, UNIT) == 0))
        def _():
            finish(late // UNIT)

        return carry

    lax.fori_loop(0, STEPS + LAST + LAG, body, 0)

    @pl.when(is_end)
    def _():
        for h in range(2 * KVH):
            out[0, :, h * HD:(h + 1) * HD] = obuf[2 + h // 8, (h % 8) * 64:(h % 8 + 1) * 64, :]
        out_send().wait_send()
        for o in range(GROUP - 1):
            meta_forward(o, g).wait_send()
            for half in range(2):
                q_forward(half, o, g).wait_send()
            for kk in range(KHALF):
                part_send(kk, o, peers[o], g).wait_send()

    @pl.when(jnp.logical_not(is_end))
    def _():
        out_send().wait_recv()
        for h in range(2 * KVH):
            out[0, :, h * HD:(h + 1) * HD] = nbuf[h // 8, (h % 8) * 64:(h % 8 + 1) * 64, :]
        q_up(0, g).wait_send()

    def drain(direction):
        def each(i, carry):
            for half in range(HALVES):
                chain(direction, i, half).wait_send()
            return carry

        lax.fori_loop(0, STEPS, each, 0)
        for kk in range(KHALF):
            tail_chain(direction, kk).wait_send()

    @pl.when(z < NZ - 1)
    def _():
        drain(0)

    @pl.when(z > 0)
    def _():
        drain(1)


def local(
    tile_features, projection, queries, query_gain, key_gain,
    tile_count, tile_slot, cross_mask, prompt_length,
):
    width = tile_features.shape[2]
    weight = projection.transpose(1, 0, 2)
    mask = cross_mask.transpose(0, 2, 1)

    vmem = pl.BlockSpec(memory_space=pltpu.VMEM)
    hbm = pl.BlockSpec(memory_space=pl.ANY)
    smem = pl.BlockSpec(memory_space=pltpu.SMEM)
    dma = pltpu.SemaphoreType.DMA
    return pl.pallas_call(
        kernel,
        out_shape=jax.ShapeDtypeStruct(queries.shape, BF16),
        in_specs=[smem, smem, smem, hbm, hbm, vmem, vmem, vmem, vmem],
        out_specs=vmem,
        scratch_shapes=[
            pltpu.VMEM((UNIT, ROWS, SLOTS_HERE, width), BF16),
            pltpu.VMEM((8, SLOTS_HERE, width), BF16),
            pltpu.VMEM((UNIT, PAIRS, width), BF16),
            pltpu.VMEM((16, width), BF16),
            pltpu.VMEM((2, PAIRS, HD), F32),
            pltpu.VMEM((2, KHALF, width, 2 * HD), BF16),
            pltpu.VMEM((2, STEPS, PAIRS, 2 * HD), BF16),
            pltpu.VMEM((2, KHALF, 16, 2 * HD), BF16),
            pltpu.VMEM((GROUP, KHALF, LANES, HD), BF16),
            pltpu.VMEM((GROUP, 2 * MAXT, LANES), jnp.int32),
            pltpu.VMEM((SLOTS_HERE, LANES, HD), BF16),
            pltpu.VMEM((SLOTS_HERE, HD, LANES), F32),
            pltpu.VMEM((SLOTS_HERE, 1, LANES), F32),
            pltpu.VMEM((KHALF, GROUP, HD + 16, LANES), BF16),
            pltpu.VMEM((KHALF, GROUP, HD + 16, LANES), BF16),
            pltpu.VMEM((KHALF, LANES, HD), BF16),
            pltpu.VMEM((2, LANES, HD), BF16),
            dma((UNIT,)),
            dma,
            dma((2, KHALF)),
            dma((2, HALVES, STEPS)),
            dma((2, HALVES, STEPS)),
            dma((2, KHALF)),
            dma((2, KHALF)),
            dma,
            dma,
            dma((2, GROUP - 1)),
            dma((2, GROUP - 1)),
            dma((GROUP - 1,)),
            dma((GROUP - 1,)),
            dma((KHALF, GROUP - 1)),
            dma((KHALF, GROUP - 1)),
            dma,
            dma,
        ],
        compiler_params=pltpu.CompilerParams(
            collective_id=0, has_side_effects=True, vmem_limit_bytes=58 * 1024 * 1024
        ),
        cost_estimate=pl.CostEstimate(
            flops=30_000_000_000, bytes_accessed=25_000_000, transcendentals=7_000_000
        ),
    )(
        tile_count, tile_slot, prompt_length, tile_features.transpose(1, 0, 2), weight, queries,
        query_gain.reshape(1, HD), key_gain.reshape(1, HD), mask,
    )


def solution(mesh):
    in_specs = (
        P("dp", None, "head"),
        P("head", None, None),
        P("dp", None, "head"),
        P(),
        P(),
        P("dp"),
        P("dp", None),
        P("dp", None, None),
        P("dp"),
    )
    out_specs = P("dp", None, "head")
    return jax.shard_map(local, mesh=mesh, in_specs=in_specs, out_specs=out_specs, check_vma=False)
```

```python
import math

import jax
import jax.numpy as jnp
from jax import lax
from jax.experimental import pallas as pl
from jax.experimental.pallas import tpu as pltpu
from jax.sharding import PartitionSpec as P

HEADS = 64
KVH = 8
HD = 128
MAXT = 4
GROUP = 4
NZ = 4
SLOTS_HERE = 2
ROWS = 160
UNIT = 10
LANES = 512
AHEAD = 3
HALVES = 2
LAG = 5
KHALF = KVH // 2
PAIRS = ROWS * SLOTS_HERE
PIECE = PAIRS // HALVES
STEPS = KHALF * UNIT
LAST = NZ - 1 + AHEAD
MESH = pl.DeviceIdType.MESH
F32 = jnp.float32
BF16 = jnp.bfloat16


def weight_head(direction, kk):
    return jnp.where(direction == 0, KHALF + kk, (kk + 2) % KHALF)


def kernel(
    count, slots, length, feat, weight, query, qgain, kgain, mask, out,
    fraw, traw, fbuf, tail, kvf, wbuf, acc, tacc, qall, mall, qcur, parts, num, den, sbuf, rbuf, obuf, nbuf,
    fsem, xsem, wsem, csend, crecv, tsend, trecv, qzs, qzr, qfs, qfr, ms, mr, ss, sr, os_, or_,
):
    dp = lax.axis_index("dp")
    z = lax.axis_index("head")
    g = lax.rem(dp, GROUP)
    base = dp - g
    is_end = (z == 0) | (z == NZ - 1)
    peers = [lax.rem(g + o, GROUP) for o in range(1, GROUP)]
    sources = [lax.rem(g + GROUP - o, GROUP) for o in range(1, GROUP)]
    beside = jnp.where(z == 0, 1, jnp.where(z == 1, 0, jnp.where(z == 2, 3, 2)))
    final = jnp.where(z == 0, 1, 0)

    def weight_copy(direction, kk):
        return pltpu.make_async_copy(
            weight.at[weight_head(direction, kk)], wbuf.at[direction, kk], wsem.at[direction, kk]
        )

    def feat_copy(i):
        return pltpu.make_async_copy(
            feat.at[pl.ds(i * ROWS, ROWS)], fraw.at[i], fsem.at[i]
        )

    def tail_copy():
        return pltpu.make_async_copy(
            feat.at[pl.ds(UNIT * ROWS, 1)], traw.at[pl.ds(0, 1)], xsem
        )

    near = jnp.where(z < NZ // 2, 0, 1)
    weight_copy(near, 0).start()
    traw[...] = jnp.zeros_like(traw)
    tail_copy().start()
    feat_copy(0).start()
    weight_copy(1 - near, 0).start()

    barrier = pltpu.get_barrier_semaphore()
    for p in peers:
        pl.semaphore_signal(barrier, inc=1, device_id={"dp": base + p}, device_id_type=MESH)

    @pl.when(z > 0)
    def _():
        pl.semaphore_signal(barrier, inc=1, device_id={"head": z - 1}, device_id_type=MESH)

    @pl.when(z < NZ - 1)
    def _():
        pl.semaphore_signal(barrier, inc=1, device_id={"head": z + 1}, device_id_type=MESH)

    tile = lax.broadcasted_iota(jnp.int32, (MAXT, LANES), 0)
    prompt = lax.rem(lax.broadcasted_iota(jnp.int32, (MAXT, LANES), 1), 64)
    seen = jnp.concatenate([mask[0]] * (LANES // 64), axis=1)
    used = (seen == 1) & (tile < count[0]) & (prompt < length[0])
    held = jnp.full((MAXT, LANES), -1, jnp.int32)
    for i in range(MAXT):
        held = jnp.where((tile == i) & (tile < count[0]), slots[0, i], held)
    mall[g, :MAXT] = jnp.where(used, 1, 0)
    mall[g, MAXT:] = held

    @pl.when(is_end)
    def _():
        pl.semaphore_wait(barrier, GROUP)

    @pl.when(jnp.logical_not(is_end))
    def _():
        pl.semaphore_wait(barrier, GROUP + 1)

    def q_up(dst_half, row):
        return pltpu.make_async_remote_copy(
            src_ref=qall.at[row, pl.ds(2, 2)], dst_ref=qall.at[row, pl.ds(dst_half, 2)],
            send_sem=qzs, recv_sem=qzr, device_id={"head": beside}, device_id_type=MESH,
        )

    def q_forward(half, o, row):
        return pltpu.make_async_remote_copy(
            src_ref=qall.at[row, pl.ds(2 * half, 2)], dst_ref=qall.at[row, pl.ds(2 * half, 2)],
            send_sem=qfs.at[half, o], recv_sem=qfr.at[half, o],
            device_id={"dp": base + peers[o]}, device_id_type=MESH,
        )

    def meta_forward(o, row):
        return pltpu.make_async_remote_copy(
            src_ref=mall.at[row], dst_ref=mall.at[row], send_sem=ms.at[o], recv_sem=mr.at[o],
            device_id={"dp": base + peers[o]}, device_id_type=MESH,
        )

    def part_send(kk, o, src_row, dst_row):
        return pltpu.make_async_remote_copy(
            src_ref=sbuf.at[kk, src_row], dst_ref=rbuf.at[kk, dst_row],
            send_sem=ss.at[kk, o], recv_sem=sr.at[kk, o],
            device_id={"dp": base + peers[o]}, device_id_type=MESH,
        )

    def out_send():
        return pltpu.make_async_remote_copy(
            src_ref=obuf.at[pl.ds(0, 2)], dst_ref=nbuf, send_sem=os_, recv_sem=or_,
            device_id={"head": beside}, device_id_type=MESH,
        )

    for i in range(1, UNIT):
        feat_copy(i).start()
    for kk in range(1, KHALF):
        for direction in range(2):
            weight_copy(direction, kk).start()

    def send_queries():
        for h in range(2 * KVH):
            block = query[0, :, h * HD:(h + 1) * HD].astype(F32)
            squares = jnp.mean(block * block, axis=-1, keepdims=True)
            normed = block * lax.rsqrt(squares + 1e-05) * qgain[...]
            qall[g, 2 + h // 8, (h % 8) * 64:(h % 8 + 1) * 64, :] = normed.astype(BF16)

        @pl.when(jnp.logical_not(is_end))
        def _():
            q_up(0, g).start()

        @pl.when(is_end)
        def _():
            for o in range(GROUP - 1):
                meta_forward(o, g).start()
                q_forward(1, o, g).start()

    def chain(direction, i, half):
        step = jnp.where(direction == 0, 1, -1)
        rows = pl.ds(half * PIECE, PIECE)
        return pltpu.make_async_remote_copy(
            src_ref=acc.at[direction, i, rows], dst_ref=acc.at[direction, i, rows],
            send_sem=csend.at[direction, half, i], recv_sem=crecv.at[direction, half, i],
            device_id={"head": z + step}, device_id_type=MESH,
        )

    def tail_chain(direction, kk):
        step = jnp.where(direction == 0, 1, -1)
        return pltpu.make_async_remote_copy(
            src_ref=tacc.at[direction, kk], dst_ref=tacc.at[direction, kk],
            send_sem=tsend.at[direction, kk], recv_sem=trecv.at[direction, kk],
            device_id={"head": z + step}, device_id_type=MESH,
        )

    def multiply(place, direction, i):
        parts[place] = jnp.dot(
            fbuf[lax.rem(i, UNIT)], wbuf[direction, i // UNIT], preferred_element_type=F32
        )

    def add_link(place, direction, i):
        first = z == jnp.where(direction == 0, 0, NZ - 1)
        last = z == jnp.where(direction == 0, NZ - 1, 0)
        kk = i // UNIT

        for half in range(HALVES):
            rows = slice(half * PIECE, (half + 1) * PIECE)

            @pl.when(first)
            def _():
                acc[direction, i, rows] = parts[place, rows].astype(BF16)

            @pl.when(jnp.logical_not(first))
            def _():
                chain(direction, i, half).wait_recv()
                held_sum = acc[direction, i, rows].astype(F32)
                acc[direction, i, rows] = (held_sum + parts[place, rows]).astype(BF16)

            @pl.when(jnp.logical_not(last))
            def _():
                chain(direction, i, half).start()

        @pl.when(lax.rem(i, UNIT) == 0)
        def _():
            part = jnp.dot(tail[...], wbuf[direction, kk], preferred_element_type=F32)

            @pl.when(first)
            def _():
                tacc[direction, kk] = part.astype(BF16)

            @pl.when(jnp.logical_not(first))
            def _():
                tail_chain(direction, kk).wait_recv()
                tacc[direction, kk] = (tacc[direction, kk].astype(F32) + part).astype(BF16)

            @pl.when(jnp.logical_not(last))
            def _():
                tail_chain(direction, kk).start()

    def weigh(kv, s, valid):
        keys = kv[:, :HD]
        squares = jnp.mean(keys * keys, axis=-1, keepdims=True)
        normed = (keys * lax.rsqrt(squares + 1e-05) * kgain[...]).astype(BF16)
        scores = lax.dot_general(
            normed, qcur[s], (((1,), (1,)), ((), ())), preferred_element_type=F32
        ) * (1.0 / math.sqrt(HD))
        weights = jnp.exp(scores)
        if valid is not None:
            weights = jnp.where(valid, weights, 0.0)
        weights = weights.astype(BF16)
        denominator = jnp.sum(weights.astype(F32), axis=0, keepdims=True)
        numerator = lax.dot_general(
            kv[:, HD:].astype(BF16), weights, (((0,), (0,)), ((), ())), preferred_element_type=F32
        )
        return numerator, denominator

    def hits(j, s):
        rows = mall[j]
        hit = jnp.where(rows[MAXT:2 * MAXT] == dp * SLOTS_HERE + s, 1, 0)
        match = jnp.max(hit, axis=0, keepdims=True)
        usable = jnp.max(hit * rows[:MAXT], axis=0, keepdims=True)
        return match, usable

    def attend(d):
        kk = d // UNIT

        @pl.when(lax.rem(d, UNIT) == 0)
        def _():
            row = lax.broadcasted_iota(jnp.int32, (16, LANES), 0)
            for s in range(SLOTS_HERE):
                chosen = jnp.zeros((LANES, HD), F32)
                for j in range(GROUP):
                    match, _u = hits(j, s)
                    chosen = chosen + match[:, :HD].astype(F32) * qall[j, kk].astype(F32)
                qcur[s] = chosen.astype(BF16)
                n0, d0 = weigh(tacc[final, kk].astype(F32), s, row == s)
                num[s] = n0
                den[s] = d0

        kvf[0] = acc[final, d, :, :HD].astype(F32)
        kvf[1] = acc[final, d, :, HD:].astype(F32)
        for s in range(SLOTS_HERE):
            every = pl.ds(s, ROWS, stride=SLOTS_HERE)
            own = jnp.concatenate([kvf[0, every, :], kvf[1, every, :]], axis=1)
            n1, d1 = weigh(own, s, None)
            num[s] += n1
            den[s] += d1

        @pl.when(lax.rem(d, UNIT) == UNIT - 1)
        def _():
            row = lax.broadcasted_iota(jnp.int32, (16, LANES), 0)
            for o in (1, 0, 2, None):
                j = g if o is None else peers[o]
                total = jnp.zeros((HD, LANES), F32)
                below = jnp.zeros((1, LANES), F32)
                for s in range(SLOTS_HERE):
                    _m, usable = hits(j, s)
                    total = total + jnp.where(usable == 1, num[s], 0.0)
                    below = below + jnp.where(usable == 1, den[s], 0.0)
                high = below.astype(BF16).astype(F32)
                pair = jnp.where(row == 0, high, jnp.where(row == 1, below - high, 0.0))
                sbuf[kk, j, :HD, :] = total.astype(BF16)
                sbuf[kk, j, HD:, :] = pair.astype(BF16)
                if o is not None:
                    part_send(kk, o, j, g).start()

    def finish(kk):
        for o in range(GROUP - 1):
            part_send(kk, o, sources[o], sources[o]).wait_recv()
        total = sbuf[kk, g].astype(F32)
        for o in range(GROUP - 1):
            total = total + rbuf[kk, sources[o]].astype(F32)
        below = total[HD:HD + 1] + total[HD + 1:HD + 2]
        live = jnp.max(mall[g][:MAXT], axis=0, keepdims=True) == 1
        inverse = 1.0 / jnp.where(live, below, 1.0)
        result = jnp.where(live, total[:HD] * inverse, 0.0)
        obuf[kk] = result.T.astype(BF16)

        @pl.when(kk == 1)
        def _():
            out_send().start()

    def load(t):
        @pl.when(t < UNIT)
        def _():
            feat_copy(t).wait()
            fbuf[t] = fraw[t].reshape(PAIRS, fraw.shape[-1])

        @pl.when(t == 0)
        def _():
            tail_copy().wait()
            tail[...] = traw[...].reshape(16, traw.shape[-1])

        for kk in range(KHALF):
            @pl.when(t == kk * UNIT)
            def _():
                for direction in range(2):
                    weight_copy(direction, kk).wait()

    def indices(t):
        near_hop = jnp.where(is_end, 0, 1)
        first_i = t - jnp.where(is_end, 0, AHEAD + 1)
        other_i = t - (AHEAD + NZ - 1 - near_hop)
        return first_i, other_i

    def prepare(t):
        load(t)
        first_i, other_i = indices(t)

        @pl.when((first_i >= 0) & (first_i < STEPS))
        def _():
            multiply(0, near, first_i)

        @pl.when((other_i >= 0) & (other_i < STEPS))
        def _():
            multiply(1, 1 - near, other_i)

    def body(t, carry):
        first_i, other_i = indices(t)
        d = t - LAST

        @pl.when((first_i >= 0) & (first_i < STEPS))
        def _():
            add_link(0, near, first_i)

        @pl.when((other_i >= 0) & (other_i < STEPS))
        def _():
            add_link(1, 1 - near, other_i)

        @pl.when(t == 1)
        def _():
            send_queries()

        @pl.when(is_end & (t == 3))
        def _():
            q_up(0, g).wait_recv()
            for o in range(GROUP - 1):
                q_forward(0, o, g).start()

        @pl.when(is_end & (d == 0))
        def _():
            for o in range(GROUP - 1):
                meta_forward(o, sources[o]).wait_recv()
                for half in range(2):
                    q_forward(half, o, sources[o]).wait_recv()

        @pl.when(is_end & (d >= 0) & (d < STEPS))
        def _():
            attend(d)

        late = d - UNIT - LAG + 1

        @pl.when(is_end & (late >= 0) & (lax.rem(late + UNIT, UNIT) == 0))
        def _():
            finish(late // UNIT)

        prepare(t + 1)
        return carry

    prepare(jnp.int32(0))
    lax.fori_loop(0, STEPS + LAST + LAG, body, 0)

    @pl.when(is_end)
    def _():
        for h in range(2 * KVH):
            out[0, :, h * HD:(h + 1) * HD] = obuf[2 + h // 8, (h % 8) * 64:(h % 8 + 1) * 64, :]
        out_send().wait_send()
        for o in range(GROUP - 1):
            meta_forward(o, g).wait_send()
            for half in range(2):
                q_forward(half, o, g).wait_send()
            for kk in range(KHALF):
                part_send(kk, o, peers[o], g).wait_send()

    @pl.when(jnp.logical_not(is_end))
    def _():
        out_send().wait_recv()
        for h in range(2 * KVH):
            out[0, :, h * HD:(h + 1) * HD] = nbuf[h // 8, (h % 8) * 64:(h % 8 + 1) * 64, :]
        q_up(0, g).wait_send()

    def drain(direction):
        def each(i, carry):
            for half in range(HALVES):
                chain(direction, i, half).wait_send()
            return carry

        lax.fori_loop(0, STEPS, each, 0)
        for kk in range(KHALF):
            tail_chain(direction, kk).wait_send()

    @pl.when(z < NZ - 1)
    def _():
        drain(0)

    @pl.when(z > 0)
    def _():
        drain(1)


def local(
    tile_features, projection, queries, query_gain, key_gain,
    tile_count, tile_slot, cross_mask, prompt_length,
):
    width = tile_features.shape[2]
    weight = projection.transpose(1, 0, 2)
    mask = cross_mask.transpose(0, 2, 1)

    vmem = pl.BlockSpec(memory_space=pltpu.VMEM)
    hbm = pl.BlockSpec(memory_space=pl.ANY)
    smem = pl.BlockSpec(memory_space=pltpu.SMEM)
    dma = pltpu.SemaphoreType.DMA
    return pl.pallas_call(
        kernel,
        out_shape=jax.ShapeDtypeStruct(queries.shape, BF16),
        in_specs=[smem, smem, smem, hbm, hbm, vmem, vmem, vmem, vmem],
        out_specs=vmem,
        scratch_shapes=[
            pltpu.VMEM((UNIT, ROWS, SLOTS_HERE, width), BF16),
            pltpu.VMEM((8, SLOTS_HERE, width), BF16),
            pltpu.VMEM((UNIT, PAIRS, width), BF16),
            pltpu.VMEM((16, width), BF16),
            pltpu.VMEM((2, PAIRS, HD), F32),
            pltpu.VMEM((2, KHALF, width, 2 * HD), BF16),
            pltpu.VMEM((2, STEPS, PAIRS, 2 * HD), BF16),
            pltpu.VMEM((2, KHALF, 16, 2 * HD), BF16),
            pltpu.VMEM((GROUP, KHALF, LANES, HD), BF16),
            pltpu.VMEM((GROUP, 2 * MAXT, LANES), jnp.int32),
            pltpu.VMEM((SLOTS_HERE, LANES, HD), BF16),
            pltpu.VMEM((2, PAIRS, 2 * HD), F32),
            pltpu.VMEM((SLOTS_HERE, HD, LANES), F32),
            pltpu.VMEM((SLOTS_HERE, 1, LANES), F32),
            pltpu.VMEM((KHALF, GROUP, HD + 16, LANES), BF16),
            pltpu.VMEM((KHALF, GROUP, HD + 16, LANES), BF16),
            pltpu.VMEM((KHALF, LANES, HD), BF16),
            pltpu.VMEM((2, LANES, HD), BF16),
            dma((UNIT,)),
            dma,
            dma((2, KHALF)),
            dma((2, HALVES, STEPS)),
            dma((2, HALVES, STEPS)),
            dma((2, KHALF)),
            dma((2, KHALF)),
            dma,
            dma,
            dma((2, GROUP - 1)),
            dma((2, GROUP - 1)),
            dma((GROUP - 1,)),
            dma((GROUP - 1,)),
            dma((KHALF, GROUP - 1)),
            dma((KHALF, GROUP - 1)),
            dma,
            dma,
        ],
        compiler_params=pltpu.CompilerParams(
            collective_id=0, has_side_effects=True, vmem_limit_bytes=58 * 1024 * 1024
        ),
        cost_estimate=pl.CostEstimate(
            flops=30_000_000_000, bytes_accessed=25_000_000, transcendentals=7_000_000
        ),
    )(
        tile_count, tile_slot, prompt_length, tile_features.transpose(1, 0, 2), weight, queries,
        query_gain.reshape(1, HD), key_gain.reshape(1, HD), mask,
    )


def solution(mesh):
    in_specs = (
        P("dp", None, "head"),
        P("head", None, None),
        P("dp", None, "head"),
        P(),
        P(),
        P("dp"),
        P("dp", None),
        P("dp", None, None),
        P("dp"),
    )
    out_specs = P("dp", None, "head")
    return jax.shard_map(local, mesh=mesh, in_specs=in_specs, out_specs=out_specs, check_vma=False)
```
